32 devices in a mesh: star: 4 (over y, core), cad: 8 (over z, x).
Axes of the slice: x: 2, y: 2, z: 4, core: 2. Of those that a mesh axis runs over, the one named last changes fastest.
Arguments:
- light: float32 [16384, 2048], P('star', 'cad'), may hold values from -2000 to 2000
- quality: int32 [2048], P('cad'), may hold values 0 or 1
- star_factors: float32 [16384, 128], P('star', 'cad'), may hold values from -6 to 6
- cadence_factors: float32 [2048, 128], P('cad', 'star'), may hold values from -6 to 6
Outputs:
- star_gradient: float32 [16384, 128], P('star', 'cad')
- cadence_gradient: float32 [2048, 128], P('cad', 'star')
- loss: float32 [], replicated
The draws below stay inside these ranges and needn't reach their ends.
All inputs are finite; a program needn't handle non-finite values. No bound on the sum of `quality` on one device may be relied on, other than what follows from the above.
Results may differ from the reference program's by a relative error of at most 0.0003.
Values sent between devices are 32-bit elements; how exact they have to be, the bound alone decides.
No kernel may reach another device: no remote copies, remote signals or barrier semaphores. Data moves between devices by JAX's collectives and lax.ppermute only.
A program may use at most 64 MiB of HBM per device.

```python
import jax
import jax.numpy as jnp
from jax import lax

RANK = 128
STARS = 16384
CADS = 2048


def draw_light(key, part):
    keys = jax.random.split(key, 6)
    star_pos = jnp.arange(STARS, dtype=jnp.float32)[:, None] / STARS
    row_scale = jnp.exp(jnp.log(10.0) * star_pos + 0.5 * jax.random.uniform(keys[1], (STARS, 1), jnp.float32))
    col_scale = jnp.exp(jnp.log(4.0) * jax.random.uniform(keys[2], (1, CADS), jnp.float32))
    period = jax.random.randint(keys[3], (STARS, 1), 40, 400)
    phase = jax.random.randint(keys[4], (STARS, 1), 0, 400)
    cadence = jnp.arange(CADS, dtype=jnp.int32)[None, :]
    transit = ((cadence + phase) % period < 12).astype(jnp.float32)
    depth = jax.random.uniform(keys[5], (STARS, 1), jnp.float32, 1.0, 4.0)
    noise = jax.random.normal(keys[0], (STARS, CADS), jnp.float32)
    noise = jnp.clip(noise, -6.0, 6.0)
    values = row_scale * (col_scale * noise - depth * transit)
    return values.astype(jnp.float32)


def plant(array, own_key, low, high):
    index_at = [jax.random.randint(jax.random.fold_in(own_key, axis), (), 0, length) for axis, length in enumerate(array.shape)]
    main_axis = array.shape.index(max(array.shape))
    next_to = index_at[:main_axis] + [(index_at[main_axis] + 1) % array.shape[main_axis]] + index_at[main_axis + 1:]
    return array.at[tuple(index_at)].set(low).at[tuple(next_to)].set(high)


def level_of(stream_key, shape, cuts, low, largest):
    factor_of = 1.0
    for position, blocks in cuts:
        draws = jax.random.uniform(jax.random.fold_in(jax.random.fold_in(stream_key, 6), position), (blocks,), jnp.float32, low / len(cuts), largest / len(cuts))
        factor_of = factor_of * jnp.repeat(jnp.exp(draws), shape[position] // blocks).reshape((-1,) + (1,) * (len(shape) - 1 - position))
    return factor_of


def scatter_about(rng, dims, scale, bound, cuts=(), kind=jnp.bfloat16):
    values = scale * jax.random.normal(rng, dims, jnp.float32)
    if cuts:
        values = values * level_of(rng, dims, cuts, -0.22, 0.18)
    return jnp.clip(values, -bound, bound).astype(kind)


def setup_inputs(seed: int = 0) -> dict:
    key_of = jax.random.split(jax.random.key(seed), 5)
    light = draw_light(jax.random.fold_in(key_of[4], 71), 0)
    quality = plant((jax.random.randint(key_of[1], (CADS,), 0, 8) < 7).astype(jnp.int32), jax.random.fold_in(key_of[1], 1), 0, 1)
    star_factors = scatter_about(key_of[2], (STARS, RANK), 1.0, 6.0, ((0, 4), (1, 8)), jnp.float32)
    cadence_factors = scatter_about(key_of[3], (CADS, RANK), 1.0, 6.0, ((0, 8), (1, 4)), jnp.float32)
    return dict(light=light, quality=quality, star_factors=star_factors, cadence_factors=cadence_factors)


def reference(light, quality, star_factors, cadence_factors):
    total_stars = light.shape[0]
    total_cads = light.shape[1]
    block = min(4096, total_stars)
    count = total_stars // block
    good = quality.astype(jnp.float32)[None, :]
    light_blocks = light.reshape(count, block, total_cads)
    factor_blocks = star_factors.reshape(count, block, star_factors.shape[1])

    def one_block(carry, pieces):
        cad_sum, loss_sum = carry
        rows, loads = pieces
        predicted = jnp.dot(loads, cadence_factors.T, precision=lax.Precision.HIGHEST, preferred_element_type=jnp.float32)
        residual = rows - predicted
        ratio = 1.0 + (residual * 0.5) ** 2
        weighted = good * residual / ratio
        star_part = -jnp.dot(weighted, cadence_factors, precision=lax.Precision.HIGHEST, preferred_element_type=jnp.float32) / jnp.sqrt(jnp.float32(total_cads))
        cad_sum = cad_sum + jnp.dot(weighted.T, loads, precision=lax.Precision.HIGHEST, preferred_element_type=jnp.float32)
        loss_sum = loss_sum + jnp.sum(good * 2.0 * jnp.log(ratio))
        return ((cad_sum, loss_sum), star_part)
    start = (jnp.zeros(cadence_factors.shape, jnp.float32), jnp.zeros((), jnp.float32))
    (cad_sum, loss_sum), star_parts = lax.scan(one_block, start, (light_blocks, factor_blocks))
    star_gradient = star_parts.reshape(star_factors.shape)
    cadence_gradient = -cad_sum / jnp.sqrt(jnp.float32(total_stars))
    loss = loss_sum / (jnp.float32(total_stars) * jnp.float32(total_cads))
    return (star_gradient, cadence_gradient, loss)
```

```python
import functools

import jax
import jax.numpy as jnp
from jax import lax
from jax.experimental import pallas as pl
from jax.experimental.pallas import tpu as pltpu
from jax.sharding import PartitionSpec as P

F32 = jnp.float32
BF16 = jnp.bfloat16


def two(x):
    hi = x.astype(BF16)
    return hi, (x - hi.astype(F32)).astype(BF16)


def three(x):
    hi = x.astype(BF16)
    rest = x - hi.astype(F32)
    mid = rest.astype(BF16)
    return hi, mid, (rest - mid.astype(F32)).astype(BF16)


def mm(a, b, ca, cb):
    return lax.dot_general(a, b, (((ca,), (cb,)), ((), ())), preferred_element_type=F32)


def body(scale, cad_scale, star_slots, cad_slots, n_star, n_cad, *refs):
    stars, cads = refs[:n_star], refs[n_star : n_star + n_cad]
    light, quality = refs[n_star + n_cad : n_star + n_cad + 2]
    outs = refs[n_star + n_cad + 2 :]
    star_out, cad_out, loss_out = outs[:n_star], outs[n_star : n_star + n_cad], outs[n_star + n_cad]
    whole, c3, cg, acc, lacc = outs[n_star + n_cad + 1 :]
    step = pl.program_id(0)
    rows = stars[0].shape[0]
    crows = cads[0].shape[0]
    rank = rows * n_star

    @pl.when(step == 0)
    def _():
        for k, ref in enumerate(cads):
            whole[pl.ds(pl.multiple_of(cad_slots(k) * crows, crows), crows), :] = ref[...]
        good = quality[...].astype(F32)
        for k in range(n_star):
            block = whole[pl.ds(pl.multiple_of(star_slots(k) * rows, rows), rows), :]
            hi, mid, lo = three(block)
            at = pl.ds(k * rows, rows)
            c3[0, at, :], c3[1, at, :], c3[2, at, :] = hi, mid, lo
            ghi, glo = two(block * (good * scale))
            cg[0, at, :], cg[1, at, :] = ghi, glo
        acc[...] = jnp.zeros_like(acc)
        lacc[...] = jnp.zeros_like(lacc)

    s = jnp.concatenate([r[...] for r in stars], 0)
    st = s.T
    hi, mid, lo = three(st)
    chi, cmid, clo = c3[0], c3[1], c3[2]
    right = jnp.concatenate([chi, cmid], 0)
    pred = (
        mm(jnp.concatenate([hi, lo], 1), jnp.concatenate([clo, chi], 0), 1, 0)
        + mm(jnp.concatenate([mid, mid], 1), right, 1, 0)
        + mm(jnp.concatenate([hi, hi], 1), right, 1, 0)
    )
    residual = light[...] - pred
    ratio = 1.0 + (residual * 0.5) ** 2
    weighted = residual / ratio
    whi, wlo = two(weighted)
    g = cg[...]
    both = mm(jnp.concatenate([g[0], g[1]], 0), whi, 1, 1)
    term = both[:rank] + both[rank:] + mm(g[0], wlo, 1, 1)
    for k, ref in enumerate(star_out):
        ref[...] = term[k * rows : (k + 1) * rows]
    shi, slo = two(s)
    both = mm(jnp.concatenate([shi, slo], 0), whi, 1, 0)
    acc[...] += both[:rank] + both[rank:] + mm(shi, wlo, 1, 0)
    n = ratio.shape[0] // 4
    prod = (ratio[:n] * ratio[n : 2 * n]) * (ratio[2 * n : 3 * n] * ratio[3 * n :])
    lacc[...] += jnp.sum(jnp.log(prod).reshape(n // 8, 8, -1), 0)

    @pl.when(step == pl.num_programs(0) - 1)
    def _():
        good = quality[...].astype(F32)
        for k in range(n_star):
            whole[pl.ds(pl.multiple_of(star_slots(k) * rows, rows), rows), :] = acc[k * rows : (k + 1) * rows]
        for k, ref in enumerate(cad_out):
            ref[...] = whole[pl.ds(pl.multiple_of(cad_slots(k) * crows, crows), crows), :] * (good * cad_scale)
        loss_out[...] = lacc[...] * good


def compute(pieces, cads, light, quality, scale, cad_scale, star_slots, cad_slots, chunk, chunks):
    rows, n = pieces[0].shape
    crows, nc = cads[0].shape
    rank = rows * len(pieces)
    bs = min(2048, n)
    first = chunk * (n // bs)
    const = lambda shape: pl.BlockSpec(shape, lambda i: (0, 0))
    piece = pl.BlockSpec((rows, bs), lambda i: (0, i))
    return pl.pallas_call(
        functools.partial(body, scale, cad_scale, star_slots, cad_slots, len(pieces), len(cads)),
        grid=(n // bs,),
        in_specs=[piece] * len(pieces) + [const((crows, nc))] * len(cads) + [pl.BlockSpec((bs, nc), lambda i: (first + i, 0)), const((1, nc))],
        out_specs=[piece] * len(pieces) + [const((crows, nc))] * len(cads) + [const((8, nc))],
        out_shape=[jax.ShapeDtypeStruct((rows, n), F32)] * len(pieces)
        + [jax.ShapeDtypeStruct((crows, nc), F32)] * len(cads) + [jax.ShapeDtypeStruct((8, nc), F32)],
        scratch_shapes=[pltpu.VMEM((rank, nc), F32), pltpu.VMEM((3, rank, nc), BF16), pltpu.VMEM((2, rank, nc), BF16),
                        pltpu.VMEM((rank, nc), F32), pltpu.VMEM((8, nc), F32)],
        compiler_params=pltpu.CompilerParams(vmem_limit_bytes=32 << 20),
    )(*pieces, *cads, light, quality)


CHUNKS = 1


def ring_order(n):
    return list(range(0, n, 2)) + list(range(1, n, 2))[::-1]


def shift(x, order, by):
    n = len(order)
    return lax.ppermute(x, "cad", [(order[p], order[(p + by) % n]) for p in range(n)])


def swap(x, axis, bit):
    return lax.ppermute(x, axis, [(i, i ^ bit) for i in range(lax.axis_size(axis))])


def ring_program(light, quality, star_t, cad_t):
    n, m = lax.axis_size("cad"), lax.axis_size("star")
    order = ring_order(n)
    stars = star_t.shape[1]
    width = stars // CHUNKS
    scale = -1.0 / float(light.shape[1] * n) ** 0.5
    cad_scale = -1.0 / float(stars * m) ** 0.5

    def star_slots(k):
        me = lax.axis_index("cad")
        place = jnp.where(me % 2 == 0, me // 2, n - 1 - me // 2)
        source = lax.rem(place + (n - k), n)
        return jnp.where(source < n // 2, 2 * source, 2 * (n - 1 - source) + 1)

    def cad_slots(k):
        return jnp.bitwise_xor(lax.axis_index("star"), k)

    with jax.named_scope("gather_cadence_factors"):
        cads = [cad_t]
        bit = 1
        while bit < m:
            got = swap(jnp.concatenate(cads, 0) if len(cads) > 1 else cads[0], "star", bit)
            cads = cads + [got[k * cad_t.shape[0] : (k + 1) * cad_t.shape[0]] for k in range(len(cads))]
            bit *= 2

    chunks = []
    for c in range(CHUNKS):
        own = star_t[:, c * width : (c + 1) * width]
        up = n // 2 if c % 2 == 0 else n // 2 - 1
        pieces = {0: own}
        with jax.named_scope("gather_star_factors"):
            for s in range(1, n // 2 + 1):
                if s <= up:
                    pieces[s] = shift(pieces[s - 1], order, 1)
                if s <= n - 1 - up:
                    pieces[n - s] = shift(pieces[(n - s + 1) % n], order, -1)
        chunks.append([pieces[k] for k in range(n)])

    stars_out, cads_out, loss_out = [], None, None
    for c in range(CHUNKS):
        up = n // 2 if c % 2 == 0 else n // 2 - 1
        got = compute(chunks[c], cads, light, quality.reshape(1, -1), scale, cad_scale, star_slots, cad_slots, c, CHUNKS)
        terms = got[:n]
        if cads_out is None:
            cads_out, loss_out = got[n : n + m], got[n + m]
        else:
            cads_out = [a + b for a, b in zip(cads_out, got[n : n + m])]
            loss_out = loss_out + got[n + m]
        with jax.named_scope("scatter_star_gradient"):
            upward = downward = None
            for s in range(n // 2, 0, -1):
                if s <= up:
                    mine = terms[n - s]
                    upward = shift(mine if upward is None else mine + upward, order, 1)
                if s <= n - 1 - up:
                    mine = terms[s]
                    downward = shift(mine if downward is None else mine + downward, order, -1)
            stars_out.append(terms[0] + upward + downward)

    with jax.named_scope("scatter_cadence_gradient"):
        bit = m // 2
        parts = list(cads_out)
        while bit:
            sent = swap(jnp.concatenate(parts[bit:] + [loss_out], 0), "star", bit)
            rows = cad_t.shape[0]
            parts = [parts[k] + sent[k * rows : (k + 1) * rows] for k in range(bit)]
            loss_out = loss_out + sent[bit * rows :]
            bit //= 2
        bit = 1
        while bit < n:
            loss_out = loss_out + swap(loss_out, "cad", bit)
            bit *= 2
    total = float(light.shape[0] * m) * float(light.shape[1] * n)
    loss = jnp.sum(loss_out) * (2.0 / total)
    star_gradient = stars_out[0] if CHUNKS == 1 else jnp.concatenate(stars_out, 1)
    return (star_gradient.T, parts[0].T, loss)


def whole_program(light, quality, star_t, cad_t):
    n, m = lax.axis_size("cad"), lax.axis_size("star")
    scale = -1.0 / float(light.shape[1] * n) ** 0.5
    cad_scale = -1.0 / float(light.shape[0] * m) ** 0.5
    stars = lax.all_gather(star_t, "cad", axis=0, tiled=True)
    cads = lax.all_gather(cad_t, "star", axis=0, tiled=True)
    first = lambda k: 0
    star, cad, loss = compute([stars], [cads], light, quality.reshape(1, -1), scale, cad_scale, first, first, 0, 1)
    star_gradient = lax.psum_scatter(star, "cad", scatter_dimension=0, tiled=True)
    cadence_gradient = lax.psum_scatter(cad, "star", scatter_dimension=0, tiled=True)
    total = float(light.shape[0] * m) * float(light.shape[1] * n)
    loss = lax.psum(jnp.sum(loss), ("star", "cad")) * (2.0 / total)
    return (star_gradient.T, cadence_gradient.T, loss)


def on_device(light, quality, star_factors, cadence_factors):
    n, m = lax.axis_size("cad"), lax.axis_size("star")
    ring = n % 2 == 0 and n & (n - 1) == 0 and m & (m - 1) == 0
    ring = ring and star_factors.shape[1] % 16 == 0 and cadence_factors.shape[1] % 16 == 0
    program = ring_program if ring else whole_program
    return program(light, quality, star_factors.T, cadence_factors.T)


def solution(mesh):
    in_specs = (P("star", "cad"), P("cad"), P("star", "cad"), P("cad", "star"))
    out_specs = (P("star", "cad"), P("cad", "star"), P())
    return jax.shard_map(
        on_device, mesh=mesh, in_specs=in_specs, out_specs=out_specs, check_vma=False
    )
```

```python
import functools

import jax
import jax.numpy as jnp
from jax import lax
from jax.experimental import pallas as pl
from jax.experimental.pallas import tpu as pltpu
from jax.sharding import PartitionSpec as P

F32 = jnp.float32
BF16 = jnp.bfloat16
SUB = 512


def two(x):
    hi = x.astype(BF16)
    return hi, (x - hi.astype(F32)).astype(BF16)


def three(x):
    hi = x.astype(BF16)
    rest = x - hi.astype(F32)
    mid = rest.astype(BF16)
    return hi, mid, (rest - mid.astype(F32)).astype(BF16)


def mm(a, b, ca, cb):
    return lax.dot_general(a, b, (((ca,), (cb,)), ((), ())), preferred_element_type=F32)


def rank_rows(k, rows):
    return pl.ds(pl.multiple_of(k * rows, rows), rows)


def stage_body(light_in, quality_in, cad_in, light, quality, cad, sem):
    copies = [
        pltpu.make_async_copy(cad_in, cad, sem.at[0]),
        pltpu.make_async_copy(quality_in, quality, sem.at[1]),
        pltpu.make_async_copy(light_in, light, sem.at[2]),
    ]
    for copy in copies:
        copy.start()
    for copy in copies:
        copy.wait()


def stage(light, quality, cad_t):
    given = (light, quality, cad_t)
    return pl.pallas_call(
        stage_body,
        in_specs=[pl.BlockSpec(memory_space=pl.ANY)] * 3,
        out_specs=[pl.BlockSpec(memory_space=pltpu.VMEM)] * 3,
        out_shape=[jax.ShapeDtypeStruct(x.shape, x.dtype) for x in given],
        scratch_shapes=[pltpu.SemaphoreType.DMA((3,))],
        cost_estimate=pl.CostEstimate(flops=0, bytes_accessed=1 << 10, transcendentals=0),
        compiler_params=pltpu.CompilerParams(vmem_limit_bytes=16 << 20),
    )(*given)


def body(plan, *refs):
    scale, cad_scale, star_slot, cad_slot, n_star, n_cad, offset, first, last = plan
    refs = list(refs)
    take = lambda count: [refs.pop(0) for _ in range(count)]
    light, quality = take(2)
    stars, cads = take(n_star), take(n_cad)
    before = [] if first else take(2)
    halves = [] if first else take(n_star)
    star_out = take(n_star)
    ends = take(3) if last else take(2)
    whole, c3, cg, acc, lacc = refs
    rows, width = stars[0].shape[0], light.shape[0] // (1 if first and last else 2)
    crows = cads[0].shape[0]
    rank = rows * n_star
    sub = min(SUB, width)

    good = quality[...].astype(F32)
    for k, ref in enumerate(cads):
        whole[rank_rows(cad_slot(k), crows), :] = ref[...]
    for k in range(n_star):
        block = whole[rank_rows(star_slot(k), rows), :]
        at = pl.ds(k * rows, rows)
        c3[0, at, :], c3[1, at, :], c3[2, at, :] = three(block)
        cg[at, :], cg[pl.ds(rank + k * rows, rows), :] = two(block * (good * scale))
    if first:
        acc[...] = jnp.zeros_like(acc)
        lacc[...] = jnp.zeros_like(lacc)
    else:
        acc[...] = before[0][...]
        lacc[...] = before[1][...]

    chi, cmid, clo = c3[0], c3[1], c3[2]
    upper = jnp.concatenate([chi, cmid], 0)
    crossed = jnp.concatenate([clo, chi], 0)
    g = cg[...]
    for b in range(width // sub):
        at = pl.ds(b * sub, sub)
        s = jnp.concatenate([r[:, pl.ds((offset if r.shape[1] > width else 0) + b * sub, sub)] for r in stars], 0)
        hi, mid, lo = three(s.T)
        pred = (
            mm(jnp.concatenate([hi, lo], 1), crossed, 1, 0)
            + mm(jnp.concatenate([mid, mid], 1), upper, 1, 0)
            + mm(jnp.concatenate([hi, hi], 1), upper, 1, 0)
        )
        residual = light[pl.ds(offset + b * sub, sub), :] - pred
        ratio = 1.0 + (residual * 0.5) ** 2
        whi, wlo = two(residual / ratio)
        both = mm(g, whi, 1, 1)
        term = both[:rank] + both[rank:] + mm(g[:rank], wlo, 1, 1)
        for k, ref in enumerate(star_out):
            start = ref.shape[1] // width * width - width + b * sub
            ref[:, pl.ds(start, sub)] = term[k * rows : (k + 1) * rows]
        shi, slo = two(s)
        both = mm(jnp.concatenate([shi, slo], 0), whi, 1, 0)
        acc[...] += both[:rank] + both[rank:] + mm(shi, wlo, 1, 0)
        q = sub // 4
        prod = (ratio[:q] * ratio[q : 2 * q]) * (ratio[2 * q : 3 * q] * ratio[3 * q :])
        lacc[...] += jnp.sum(jnp.log(prod).reshape(q // 8, 8, -1), 0)

    if last:
        for k in range(n_star):
            whole[rank_rows(star_slot(k), rows), :] = acc[k * rows : (k + 1) * rows]
        keep, send, loss = ends
        mine = max(n_cad // 2, 1)
        for k in range(n_cad):
            ref, place = (keep, k) if k < mine else (send, k - mine)
            ref[pl.ds(place * crows, crows), :] = whole[rank_rows(cad_slot(k), crows), :] * (good * cad_scale)
        sums = lacc[...] * good
        lanes = sum(sums[:, c : c + 128] for c in range(0, sums.shape[1], 128))
        loss[...] = lanes
        if not first:
            for ref, half in zip(star_out, halves, strict=True):
                ref[:, :width] = half[...]
                ref[:8, ref.shape[1] - 128 :] = lanes
                ref[8:, ref.shape[1] - 128 :] = jnp.zeros((rows - 8, 128), F32)
    else:
        ends[0][...] = acc[...]
        ends[1][...] = lacc[...]


def compute(stars, cads, light, quality, before, scale, cad_scale, star_slot, cad_slot, chunk, chunks):
    rows, width = stars[0].shape[0], light.shape[0] // chunks
    crows, nc = cads[0].shape
    n_star, n_cad = len(stars), len(cads)
    rank = rows * n_star
    first, last = chunk == 0, chunk == chunks - 1
    plan = (scale, cad_scale, star_slot, cad_slot, n_star, n_cad, chunk * width, first, last)
    sds = lambda *shape: jax.ShapeDtypeStruct(shape, F32)
    mine = max(n_cad // 2, 1)
    ends = [sds(crows * mine, nc), sds(crows * max(n_cad - mine, 1), nc), sds(8, 128)] if last else [sds(rank, nc), sds(8, nc)]
    given = [light, quality] + stars + cads + list(before)
    terms = [sds(rows, width if first else 2 * width + 128)] * n_star
    vmem = pl.BlockSpec(memory_space=pltpu.VMEM)
    macs = width * nc * rank
    return pl.pallas_call(
        functools.partial(body, plan),
        in_specs=[vmem] * len(given),
        out_specs=[vmem] * (n_star + len(ends)),
        out_shape=terms + ends,
        scratch_shapes=[
            pltpu.VMEM((rank, nc), F32),
            pltpu.VMEM((3, rank, nc), BF16),
            pltpu.VMEM((2 * rank, nc), BF16),
            pltpu.VMEM((rank, nc), F32),
            pltpu.VMEM((8, nc), F32),
        ],
        compiler_params=pltpu.CompilerParams(vmem_limit_bytes=32 << 20),
        cost_estimate=pl.CostEstimate(flops=24 * macs, bytes_accessed=4 * width * (nc + 2 * rank), transcendentals=width * nc),
    )(*given)


def small_call(body_of, given, shapes, limit=4):
    vmem = pl.BlockSpec(memory_space=pltpu.VMEM)
    return pl.pallas_call(
        body_of,
        in_specs=[vmem] * len(given),
        out_specs=[vmem] * len(shapes),
        out_shape=[jax.ShapeDtypeStruct(shape, F32) for shape in shapes],
        cost_estimate=pl.CostEstimate(flops=0, bytes_accessed=1 << 10, transcendentals=0),
        compiler_params=pltpu.CompilerParams(vmem_limit_bytes=limit << 20),
    )(*given)


def empty_body(*refs):
    pass


def hold(x, *after):
    anywhere = pl.BlockSpec(memory_space=pl.ANY)
    return pl.pallas_call(
        empty_body,
        in_specs=[anywhere] * (1 + len(after)),
        out_specs=anywhere,
        out_shape=jax.ShapeDtypeStruct(x.shape, x.dtype),
        input_output_aliases={0: 0},
        cost_estimate=pl.CostEstimate(flops=0, bytes_accessed=1 << 10, transcendentals=0),
        compiler_params=pltpu.CompilerParams(vmem_limit_bytes=1 << 20),
    )(x, *after)


def halve_body(keep, got, keep_out, send_out):
    rows = keep_out.shape[0]
    keep_out[...] = keep[:rows] + got[:rows]
    send_out[...] = keep[rows:] + got[rows:]


def halve(keep, got):
    shape = (keep.shape[0] // 2, keep.shape[1])
    return small_call(halve_body, [keep, got], [shape, shape])


def last_stars_body(mine, up, back, out, loss):
    width = out.shape[1]
    out[...] = mine[:, :width] + up[:, :width] + back[:, :width]
    loss[...] = mine[:8, width:] + up[:8, width:] + back[:8, width:]


def last_stars(mine, up, back):
    rows, width = mine.shape
    return small_call(last_stars_body, [mine, up, back], [(rows, width - 128), (8, 128)])


def last_loss_body(factor, *refs):
    refs[-1][...] = jnp.sum(sum(ref[...] for ref in refs[:-1]), keepdims=True) * factor


def last_loss(losses, factor):
    return small_call(functools.partial(last_loss_body, factor), losses, [(1, 1)])[0]


def ring_order(n):
    return list(range(0, n, 2)) + list(range(1, n, 2))[::-1]


def shift(x, core=0):
    m, n = lax.axis_size("star"), lax.axis_size("cad")
    order = ring_order(n)
    pairs = []
    for i in range(m):
        way = 1 if i % 2 == 0 else -1
        source, target = i ^ int(core < 0), i ^ int(core > 0)
        pairs += [(source * n + order[p], target * n + order[(p + way) % n]) for p in range(n)]
    return lax.ppermute(x, ("star", "cad"), pairs)


def swap(x, axis, bit):
    return lax.ppermute(x, axis, [(i, i ^ bit) for i in range(lax.axis_size(axis))])


def ring_program(light, quality, star_t, cad_t):
    n, m = lax.axis_size("cad"), lax.axis_size("star")
    count, nc = light.shape
    half = count // 2
    scale = -1.0 / float(nc * n) ** 0.5
    cad_scale = -1.0 / float(count * m) ** 0.5
    factor = 2.0 / (float(count * m) * float(nc * n))

    def star_slot(k):
        me = lax.axis_index("cad")
        place = jnp.where(me % 2 == 0, me // 2, n - 1 - me // 2)
        back = jnp.where(lax.axis_index("star") % 2 == 0, n - k, k)
        source = lax.rem(place + back, n)
        return jnp.where(source < n // 2, 2 * source, 2 * (n - 1 - source) + 1)

    def cad_slot(k):
        return jnp.bitwise_xor(lax.axis_index("star"), k)

    light, quality, cad_t = stage(light, quality.reshape(1, -1), cad_t)

    with jax.named_scope("gather_cadence_factors"):
        cads = [cad_t] + [swap(cad_t, "star", bit) for bit in range(1, m)]

    far = n // 2
    pieces = [star_t] + [None] * (n - 1)
    with jax.named_scope("gather_star_factors"):
        beside = swap(star_t, "star", 1)
        for s in range(1, far):
            pieces[s] = shift(pieces[s - 1])
            if s == 1:
                beside = shift(beside)
                pieces[s], beside = hold(pieces[s], light), hold(beside, light)
            elif s < far - 1:
                beside = shift(beside)
                pieces[s] = hold(pieces[s], *cads[1:])
            else:
                beside = shift(beside, 1)
            pieces[n - s] = swap(beside, "star", 1) if s < far - 1 else beside
        far_a, far_b = shift(pieces[far - 1][:, :half]), shift(pieces[far - 1][:, half:])

    pieces[far] = far_a
    got = compute(pieces, cads, light, quality, (), scale, cad_scale, star_slot, cad_slot, 0, 2)
    terms, before = got[:n], got[n:]
    pieces[far] = far_b
    got = compute(pieces, cads, light, quality, list(before) + list(terms), scale, cad_scale, star_slot, cad_slot, 1, 2)
    terms, (keep, send, loss) = got[:n], got[n:]

    with jax.named_scope("scatter_star_gradient"):
        up = shift(terms[far])
        beside = shift(swap(terms[far - 1], "star", 1))
        keep, send = halve(keep, swap(send, "star", 2))
        for s in range(far - 1, 0, -1):
            message = terms[n - s] + up
            if s < far - 1:
                message = hold(message, waiting, *([cad_gradient] if s == 1 else []))
            up = shift(message)
            if s > 1:
                waiting = hold(swap(terms[s - 1], "star", 1) + beside, message, *([keep] if s == 3 else []))
                beside = shift(waiting)
            if s == 2:
                cad_gradient = keep + swap(send, "star", 1)
        beside = swap(beside, "star", 1)
        star_gradient, loss = last_stars(terms[0], up, beside)
    with jax.named_scope("sum_loss"):
        total = last_loss([loss] + [swap(loss, "star", bit) for bit in range(1, m)], factor)
    return (star_gradient.T, cad_gradient.T, total[0, 0])


def whole_program(light, quality, star_t, cad_t):
    n, m = lax.axis_size("cad"), lax.axis_size("star")
    count, nc = light.shape
    scale = -1.0 / float(nc * n) ** 0.5
    cad_scale = -1.0 / float(count * m) ** 0.5
    stars = [lax.all_gather(star_t, "cad", axis=0, tiled=True)]
    cads = [lax.all_gather(cad_t, "star", axis=0, tiled=True)]
    first = lambda k: 0
    star, cad, _, loss = compute(stars, cads, light, quality.reshape(1, -1), (), scale, cad_scale, first, first, 0, 1)
    star_gradient = lax.psum_scatter(star, "cad", scatter_dimension=0, tiled=True)
    cadence_gradient = lax.psum_scatter(cad, "star", scatter_dimension=0, tiled=True)
    loss = lax.psum(jnp.sum(loss), ("star", "cad")) * (2.0 / (float(count * m) * float(nc * n)))
    return (star_gradient.T, cadence_gradient.T, loss)


def on_device(light, quality, star_factors, cadence_factors):
    ring = lax.axis_size("cad") == 8 and lax.axis_size("star") == 4
    program = ring_program if ring else whole_program
    return program(light, quality, star_factors.T, cadence_factors.T)


def solution(mesh):
    in_specs = (P("star", "cad"), P("cad"), P("star", "cad"), P("cad", "star"))
    out_specs = (P("star", "cad"), P("cad", "star"), P())
    return jax.shard_map(
        on_device, mesh=mesh, in_specs=in_specs, out_specs=out_specs, check_vma=False
    )
```

```python
import functools

import jax
import jax.numpy as jnp
from jax import lax
from jax.experimental import pallas as pl
from jax.experimental.pallas import tpu as pltpu
from jax.sharding import PartitionSpec as P

F32 = jnp.float32
BF16 = jnp.bfloat16
SUB = 512


def two(x):
    hi = x.astype(BF16)
    return hi, (x - hi.astype(F32)).astype(BF16)


def three(x):
    hi = x.astype(BF16)
    rest = x - hi.astype(F32)
    mid = rest.astype(BF16)
    return hi, mid, (rest - mid.astype(F32)).astype(BF16)


def mm(a, b, ca, cb):
    return lax.dot_general(a, b, (((ca,), (cb,)), ((), ())), preferred_element_type=F32)


def rank_rows(k, rows):
    return pl.ds(pl.multiple_of(k * rows, rows), rows)


def stage_body(light_in, quality_in, cad_in, light, quality, cad, sem):
    copies = [
        pltpu.make_async_copy(cad_in, cad, sem.at[0]),
        pltpu.make_async_copy(quality_in, quality, sem.at[1]),
        pltpu.make_async_copy(light_in, light, sem.at[2]),
    ]
    for copy in copies:
        copy.start()
    for copy in copies:
        copy.wait()


def stage(light, quality, cad_t):
    given = (light, quality, cad_t)
    return pl.pallas_call(
        stage_body,
        in_specs=[pl.BlockSpec(memory_space=pl.ANY)] * 3,
        out_specs=[pl.BlockSpec(memory_space=pltpu.VMEM)] * 3,
        out_shape=[jax.ShapeDtypeStruct(x.shape, x.dtype) for x in given],
        scratch_shapes=[pltpu.SemaphoreType.DMA((3,))],
        cost_estimate=pl.CostEstimate(flops=0, bytes_accessed=1 << 10, transcendentals=0),
        compiler_params=pltpu.CompilerParams(vmem_limit_bytes=16 << 20),
    )(*given)


def place_cads(whole, cads, cad_slot):
    rows = cads[0].shape[0]
    for k, ref in enumerate(cads):
        whole[rank_rows(cad_slot(k), rows), :] = ref[...]


def of_slots(whole, star_slot, slots, rows):
    return jnp.concatenate([whole[rank_rows(star_slot(k), rows), :] for k in slots], 0)


def columns(refs, start, size):
    return jnp.concatenate([ref[:, pl.ds(start, size)] for ref in refs], 0)


def product_left(s):
    hi, mid, lo = three(s)
    return jnp.concatenate([hi, lo, mid, mid, hi, hi], 0)


def product_right(c):
    hi, mid, lo = three(c)
    return jnp.concatenate([lo, hi, hi, mid, hi, mid], 0)


def early_body(plan, *refs):
    star_slot, cad_slot, slots, n_cad = plan
    light, refs = refs[0], refs[1:]
    stars, cads = refs[: len(slots)], refs[len(slots) : len(slots) + n_cad]
    out, whole = refs[-2:]
    rows = stars[0].shape[0]
    place_cads(whole, cads, cad_slot)
    pad = -rows * len(slots) % 128
    block = of_slots(whole, star_slot, slots, rows)
    if pad:
        block = jnp.concatenate([block, jnp.zeros((pad, block.shape[1]), F32)], 0)
    right = product_right(block)
    for start in range(0, light.shape[0], SUB):
        s = columns(stars, start, SUB)
        if pad:
            s = jnp.concatenate([s, jnp.zeros((pad, SUB), F32)], 0)
        hi, mid, lo = three(s.T)
        left = jnp.concatenate([hi, lo, mid, mid, hi, hi], 1)
        at = pl.ds(start, SUB)
        out[at, :] = light[at, :] - mm(left, right, 1, 0)


def cells_body(plan, *refs):
    scale, star_slot, cad_slot, late, lead, n_cad, offset, first, last = plan
    refs = list(refs)
    take = lambda count: [refs.pop(0) for _ in range(count)]
    rest, quality = take(2)
    stars, cads = take(len(late)), take(n_cad)
    before = [] if first else take(1 + len(lead))
    whi_out, wlo_out, loss_out = take(3)
    terms = take(len(lead))
    whole, lacc = refs
    width = whi_out.shape[0]
    good = quality[...].astype(F32)
    place_cads(whole, cads, cad_slot)
    rows = stars[0].shape[0] if late else 0
    right = product_right(of_slots(whole, star_slot, late, rows)) if late else None
    ghi, glo = two(of_slots(whole, star_slot, lead, rows) * (good * scale)) if lead else (None, None)
    gt = jnp.concatenate([glo.T, ghi.T, ghi.T], 0) if lead else None
    lacc[...] = jnp.zeros_like(lacc) if first else before[0][...]
    for start in range(0, width, SUB):
        at = pl.ds(start, SUB)
        residual = rest[pl.ds(offset + start, SUB), :]
        if late:
            s = jnp.concatenate([r[:, pl.ds((offset if r.shape[1] > width else 0) + start, SUB)] for r in stars], 0)
            residual = residual - mm(product_left(s), right, 0, 0)
        ratio = 1.0 + (residual * 0.5) ** 2
        whi, wlo = two(residual / ratio)
        whi_out[at, :], wlo_out[at, :] = whi, wlo
        if lead:
            term = mm(jnp.concatenate([whi, wlo, whi], 1), gt, 1, 0).T
            for k, ref in enumerate(terms):
                to = pl.ds(start if first else width + start, SUB)
                ref[:, to] = term[k * rows : (k + 1) * rows]
        q = SUB // 4
        prod = (ratio[:q] * ratio[q : 2 * q]) * (ratio[2 * q : 3 * q] * ratio[3 * q :])
        lacc[...] += jnp.sum(jnp.log(prod).reshape(q // 8, 8, -1), 0)
    if not last:
        loss_out[...] = lacc[...]
        return
    sums = lacc[...] * good
    lanes = sum(sums[:, c : c + 128] for c in range(0, sums.shape[1], 128))
    loss_out[...] = lanes
    for ref, half in zip(terms, before[1:], strict=True):
        ref[:, :width] = half[...]
        put_lanes(ref, lanes)


def put_lanes(ref, lanes):
    ref[:8, ref.shape[1] - 128 :] = lanes
    ref[8:, ref.shape[1] - 128 :] = jnp.zeros((ref.shape[0] - 8, 128), F32)


def sums_body(plan, *refs):
    scale, cad_scale, star_slot, cad_slot, slots, n_star, n_cad, chunks = plan
    refs = list(refs)
    take = lambda count: [refs.pop(0) for _ in range(count)]
    parts, loss, quality = take(2 * chunks), take(1)[0], take(1)[0]
    stars, halves, cads = take(n_star), take(chunks - 1), take(n_cad)
    outs = take(len(slots))
    keep, send, whole, acc = refs
    rows, crows = stars[0].shape[0], cads[0].shape[0]
    width = parts[0].shape[0]
    good = quality[...].astype(F32)
    place_cads(whole, cads, cad_slot)
    ghi, glo = two(of_slots(whole, star_slot, slots, rows) * (good * scale))
    gt = jnp.concatenate([glo.T, ghi.T, ghi.T], 0)
    acc[...] = jnp.zeros_like(acc)
    for c in range(chunks):
        pieces = list(stars)
        if c:
            pieces[n_star // 2] = halves[c - 1]
        for start in range(0, width, SUB):
            at = pl.ds(start, SUB)
            whi, wlo = parts[2 * c][at, :], parts[2 * c + 1][at, :]
            term = mm(jnp.concatenate([whi, wlo, whi], 1), gt, 1, 0).T
            for k, ref in enumerate(outs):
                ref[:, pl.ds(c * width + start, SUB)] = term[k * rows : (k + 1) * rows]
            s = jnp.concatenate([r[:, pl.ds((c * width if r.shape[1] > width else 0) + start, SUB)] for r in pieces], 0)
            shi, slo = two(s)
            acc[...] += mm(jnp.concatenate([slo, shi, shi], 1), jnp.concatenate([whi, wlo, whi], 0), 1, 0)
    if chunks > 1:
        for ref in outs:
            put_lanes(ref, loss[...])
    for k in range(n_star):
        whole[rank_rows(star_slot(k), rows), :] = acc[k * rows : (k + 1) * rows]
    mine = max(n_cad // 2, 1)
    for k in range(n_cad):
        ref, place = (keep, k) if k < mine else (send, k - mine)
        ref[pl.ds(place * crows, crows), :] = whole[rank_rows(cad_slot(k), crows), :] * (good * cad_scale)


def big_call(body_of, given, out_shape, scratch, macs):
    vmem = pl.BlockSpec(memory_space=pltpu.VMEM)
    return pl.pallas_call(
        body_of,
        in_specs=[vmem] * len(given),
        out_specs=[vmem] * len(out_shape),
        out_shape=out_shape,
        scratch_shapes=scratch,
        compiler_params=pltpu.CompilerParams(vmem_limit_bytes=24 << 20),
        cost_estimate=pl.CostEstimate(flops=2 * macs, bytes_accessed=1 << 20, transcendentals=0),
    )(*given)


def sds(*shape, kind=F32):
    return jax.ShapeDtypeStruct(shape, kind)


def early(light, stars, cads, star_slot, cad_slot, slots):
    count, nc = light.shape
    rank = cads[0].shape[0] * len(cads)
    plan = (star_slot, cad_slot, slots, len(cads))
    scratch = [pltpu.VMEM((rank, nc), F32)]
    return big_call(functools.partial(early_body, plan), [light] + stars + cads, [sds(count, nc)], scratch, 6 * count * nc * rank)[0]


def cells(rest, quality, stars, cads, before, scale, star_slot, cad_slot, late, lead, chunk, chunks):
    count, nc = rest.shape
    width = count // chunks
    rank = cads[0].shape[0] * len(cads)
    rows = stars[0].shape[0] if stars else 0
    first, last = chunk == 0, chunk == chunks - 1
    plan = (scale, star_slot, cad_slot, late, lead, len(cads), chunk * width, first, last)
    out = [sds(width, nc, kind=BF16)] * 2 + [sds(8, 128) if last else sds(8, nc)]
    out += [sds(rows, width if first else count + 128)] * len(lead)
    scratch = [pltpu.VMEM((rank, nc), F32), pltpu.VMEM((8, nc), F32)]
    return list(big_call(functools.partial(cells_body, plan), [rest, quality] + stars + cads + before, out, scratch, 4 * width * nc * rank))


def sums(parts, loss, quality, stars, halves, cads, scale, cad_scale, star_slot, cad_slot, slots):
    chunks, nc = len(parts) // 2, parts[0].shape[1]
    count = parts[0].shape[0] * chunks
    n_star, n_cad = len(stars), len(cads)
    rows, crows = stars[0].shape[0], cads[0].shape[0]
    rank = rows * n_star
    mine = max(n_cad // 2, 1)
    plan = (scale, cad_scale, star_slot, cad_slot, slots, n_star, n_cad, chunks)
    out = [sds(rows, count + (128 if chunks > 1 else 0))] * len(slots)
    out += [sds(crows * mine, nc), sds(crows * max(n_cad - mine, 1), nc)]
    scratch = [pltpu.VMEM((rank, nc), F32), pltpu.VMEM((rank, nc), F32)]
    given = parts + [loss, quality] + stars + halves + cads
    return list(big_call(functools.partial(sums_body, plan), given, out, scratch, 6 * count * nc * rank))


def small_call(body_of, given, shapes, limit=4):
    vmem = pl.BlockSpec(memory_space=pltpu.VMEM)
    return pl.pallas_call(
        body_of,
        in_specs=[vmem] * len(given),
        out_specs=[vmem] * len(shapes),
        out_shape=[jax.ShapeDtypeStruct(shape, F32) for shape in shapes],
        cost_estimate=pl.CostEstimate(flops=0, bytes_accessed=1 << 10, transcendentals=0),
        compiler_params=pltpu.CompilerParams(vmem_limit_bytes=limit << 20),
    )(*given)


def empty_body(*refs):
    pass


def hold(x, *after):
    anywhere = pl.BlockSpec(memory_space=pl.ANY)
    return pl.pallas_call(
        empty_body,
        in_specs=[anywhere] * (1 + len(after)),
        out_specs=anywhere,
        out_shape=jax.ShapeDtypeStruct(x.shape, x.dtype),
        input_output_aliases={0: 0},
        cost_estimate=pl.CostEstimate(flops=0, bytes_accessed=1 << 10, transcendentals=0),
        compiler_params=pltpu.CompilerParams(vmem_limit_bytes=1 << 20),
    )(x, *after)


def halve_body(keep, got, keep_out, send_out):
    rows = keep_out.shape[0]
    keep_out[...] = keep[:rows] + got[:rows]
    send_out[...] = keep[rows:] + got[rows:]


def halve(keep, got):
    shape = (keep.shape[0] // 2, keep.shape[1])
    return small_call(halve_body, [keep, got], [shape, shape])


def add_part_body(mine, got, out, part):
    out[...] = mine[...] + got[...]
    part[...] = out[:8, out.shape[1] - 128 :]


def add_part(mine, got):
    return small_call(add_part_body, [mine, got], [mine.shape, (8, 128)])


def loss_part_body(loss, near, beside, out):
    out[...] = loss[...] + near[...] + beside[:8, beside.shape[1] - 128 :]


def loss_part(loss, near, beside):
    return small_call(loss_part_body, [loss, near, beside], [(8, 128)])[0]


def last_stars_body(factor, mine, up, back, *refs):
    *losses, out, total = refs
    width = out.shape[1]
    out[...] = mine[:, :width] + up[:, :width] + back[:, :width]
    total[...] = jnp.sum(sum(ref[...] for ref in losses), keepdims=True) * factor


def last_stars(mine, up, back, losses, factor):
    rows, width = mine.shape
    shapes = [(rows, width - 128), (1, 1)]
    return small_call(functools.partial(last_stars_body, factor), [mine, up, back] + losses, shapes)


def ring_order(n):
    return list(range(0, n, 2)) + list(range(1, n, 2))[::-1]


def shift(x, core=0, places=1):
    m, n = lax.axis_size("star"), lax.axis_size("cad")
    order = ring_order(n)
    pairs = []
    for i in range(m):
        way = places if i % 2 == 0 else -places
        source, target = i ^ int(core < 0), i ^ int(core > 0)
        pairs += [(source * n + order[p], target * n + order[(p + way) % n]) for p in range(n)]
    return lax.ppermute(x, ("star", "cad"), pairs)


def swap(x, axis, bit):
    return lax.ppermute(x, axis, [(i, i ^ bit) for i in range(lax.axis_size(axis))])


def ring_program(light, quality, star_t, cad_t):
    n, m = lax.axis_size("cad"), lax.axis_size("star")
    count, nc = light.shape
    half = count // 2
    scale = -1.0 / float(nc * n) ** 0.5
    cad_scale = -1.0 / float(count * m) ** 0.5
    factor = 2.0 / (float(count * m) * float(nc * n))

    def star_slot(k):
        me = lax.axis_index("cad")
        place = jnp.where(me % 2 == 0, me // 2, n - 1 - me // 2)
        back = jnp.where(lax.axis_index("star") % 2 == 0, n - k, k)
        source = lax.rem(place + back, n)
        return jnp.where(source < n // 2, 2 * source, 2 * (n - 1 - source) + 1)

    def cad_slot(k):
        return jnp.bitwise_xor(lax.axis_index("star"), k)

    light, quality, cad_t = stage(light, quality.reshape(1, -1), cad_t)

    with jax.named_scope("gather_cadence_factors"):
        cads = [cad_t] + [swap(cad_t, "star", bit) for bit in range(1, m)]

    far = n // 2
    pieces = [star_t] + [None] * (n - 1)
    with jax.named_scope("gather_star_factors"):
        beside = swap(star_t, "star", 1)
        for s in range(1, far):
            pieces[s] = shift(pieces[s - 1])
            if s == 1:
                beside = shift(beside)
                pieces[s], beside = hold(pieces[s], light), hold(beside, light)
            elif s < far - 1:
                beside = shift(beside)
                pieces[s] = hold(pieces[s], *cads[1:])
            else:
                beside = shift(beside, 1)
            pieces[n - s] = swap(beside, "star", 1) if s < far - 1 else beside
        far_a, far_b = shift(pieces[far - 1][:, :half]), shift(pieces[far - 1][:, half:])

    slots = [k for k in range(n) if k not in (far, far + 1)]
    rest = early(light, [pieces[k] for k in slots], cads, star_slot, cad_slot, slots)
    late, lead = [far, far + 1], [far, far - 1, far - 2]
    got_a = cells(rest, quality, [far_a, pieces[far + 1]], cads, [], scale, star_slot, cad_slot, late, lead, 0, 2)
    got_b = cells(rest, quality, [far_b, pieces[far + 1]], cads, got_a[2:], scale, star_slot, cad_slot, late, lead, 1, 2)
    loss = got_b[2]
    pieces[far] = far_a
    slots = [k for k in range(n) if k not in lead]
    second, third = swap(got_b[4], "star", 1), swap(got_b[5], "star", 1)
    loss = hold(loss, second)
    got = sums(got_a[:2] + got_b[:2], loss, quality, pieces, [far_b], cads, scale, cad_scale, star_slot, cad_slot, slots)
    terms = dict(zip(lead + slots, got_b[3:] + got[:-2], strict=True))
    keep, send = got[-2:]

    with jax.named_scope("scatter_star_gradient"):
        up, beside = shift(terms[far]), shift(second)
        up = shift(terms[far + 1] + up)
        message = third + beside
        keep, send = halve(keep, swap(hold(send, message), "star", 2))
        beside = shift(message)
        up = shift(hold(terms[far + 2] + up, message))
        cad_gradient = keep + swap(send, "star", 1)
        message = hold(swap(terms[1], "star", 1) + beside, keep)
        beside = shift(message)
        message, near = add_part(terms[far + 3], hold(up, message))
        near = shift(near)
        up = shift(message)
        back = swap(hold(beside, cad_gradient), "star", 1)
        part = loss_part(loss, near, beside)
        losses = [part] + [swap(part, "star", bit) for bit in range(1, m)]
        star_gradient, total = last_stars(terms[0], up, back, losses, factor)
    return (star_gradient.T, cad_gradient.T, total[0, 0])


def whole_program(light, quality, star_t, cad_t):
    n, m = lax.axis_size("cad"), lax.axis_size("star")
    count, nc = light.shape
    scale = -1.0 / float(nc * n) ** 0.5
    cad_scale = -1.0 / float(count * m) ** 0.5
    stars = [lax.all_gather(star_t, "cad", axis=0, tiled=True)]
    cads = [lax.all_gather(cad_t, "star", axis=0, tiled=True)]
    first = lambda k: 0
    light = early(light, stars, cads, first, first, [0])
    whi, wlo, loss = cells(light, quality.reshape(1, -1), [], cads, [], scale, first, first, [], [], 0, 1)
    parts = [whi, wlo]
    star, cad, _ = sums(parts, loss, quality.reshape(1, -1), stars, [], cads, scale, cad_scale, first, first, [0])
    star_gradient = lax.psum_scatter(star, "cad", scatter_dimension=0, tiled=True)
    cadence_gradient = lax.psum_scatter(cad, "star", scatter_dimension=0, tiled=True)
    loss = lax.psum(jnp.sum(loss), ("star", "cad")) * (2.0 / (float(count * m) * float(nc * n)))
    return (star_gradient.T, cadence_gradient.T, loss)


def on_device(light, quality, star_factors, cadence_factors):
    ring = lax.axis_size("cad") == 8 and lax.axis_size("star") == 4
    program = ring_program if ring else whole_program
    return program(light, quality, star_factors.T, cadence_factors.T)


def solution(mesh):
    in_specs = (P("star", "cad"), P("cad"), P("star", "cad"), P("cad", "star"))
    out_specs = (P("star", "cad"), P("cad", "star"), P())
    return jax.shard_map(
        on_device, mesh=mesh, in_specs=in_specs, out_specs=out_specs, check_vma=False
    )
```

```python
import functools

import jax
import jax.numpy as jnp
from jax import lax
from jax.experimental import pallas as pl
from jax.experimental.pallas import tpu as pltpu
from jax.sharding import PartitionSpec as P

F32 = jnp.float32
BF16 = jnp.bfloat16
SUB = 512


def two(x):
    hi = x.astype(BF16)
    return hi, (x - hi.astype(F32)).astype(BF16)


def three(x):
    hi = x.astype(BF16)
    rest = x - hi.astype(F32)
    mid = rest.astype(BF16)
    return hi, mid, (rest - mid.astype(F32)).astype(BF16)


def mm(a, b, ca, cb):
    return lax.dot_general(a, b, (((ca,), (cb,)), ((), ())), preferred_element_type=F32)


def rank_rows(k, rows):
    return pl.ds(pl.multiple_of(k * rows, rows), rows)


def stage_body(*refs):
    count = len(refs) // 2
    sem = refs[-1]
    copies = [pltpu.make_async_copy(refs[i], refs[count + i], sem.at[i]) for i in range(count)]
    for copy in copies:
        copy.start()
    for copy in copies:
        copy.wait()


def stage(*given):
    return pl.pallas_call(
        stage_body,
        in_specs=[pl.BlockSpec(memory_space=pl.ANY)] * len(given),
        out_specs=[pl.BlockSpec(memory_space=pltpu.VMEM)] * len(given),
        out_shape=[jax.ShapeDtypeStruct(x.shape, x.dtype) for x in given],
        scratch_shapes=[pltpu.SemaphoreType.DMA((len(given),))],
        cost_estimate=pl.CostEstimate(flops=0, bytes_accessed=1 << 10, transcendentals=0),
        compiler_params=pltpu.CompilerParams(vmem_limit_bytes=16 << 20),
    )(*given)


def place_cads(whole, cads, cad_slot):
    rows = cads[0].shape[0]
    for k, ref in enumerate(cads):
        whole[rank_rows(cad_slot(k), rows), :] = ref[...]


def of_slots(whole, star_slot, slots, rows):
    return jnp.concatenate([whole[rank_rows(star_slot(k), rows), :] for k in slots], 0)


def columns(refs, start, size):
    return jnp.concatenate([ref[:, pl.ds(start, size)] for ref in refs], 0)


def product_left(s):
    hi, mid, lo = three(s)
    return jnp.concatenate([hi, lo, mid, mid, hi, hi], 0)


def product_right(c):
    hi, mid, lo = three(c)
    return jnp.concatenate([lo, hi, hi, mid, hi, mid], 0)


def early_body(plan, *refs):
    star_slot, cad_slot, slots, n_cad = plan
    light, refs = refs[0], refs[1:]
    stars, cads = refs[: len(slots)], refs[len(slots) : len(slots) + n_cad]
    out, whole = refs[-2:]
    rows = stars[0].shape[0]
    place_cads(whole, cads, cad_slot)
    pad = -rows * len(slots) % 128
    block = of_slots(whole, star_slot, slots, rows)
    if pad:
        block = jnp.concatenate([block, jnp.zeros((pad, block.shape[1]), F32)], 0)
    right = product_right(block)
    for start in range(0, light.shape[0], SUB):
        s = columns(stars, start, SUB)
        if pad:
            s = jnp.concatenate([s, jnp.zeros((pad, SUB), F32)], 0)
        hi, mid, lo = three(s.T)
        left = jnp.concatenate([hi, lo, mid, mid, hi, hi], 1)
        at = pl.ds(start, SUB)
        out[at, :] = light[at, :] - mm(left, right, 1, 0)


def cells_body(plan, *refs):
    scale, star_slot, cad_slot, late, lead, n_cad, offset, first, last = plan
    refs = list(refs)
    take = lambda count: [refs.pop(0) for _ in range(count)]
    rest, quality = take(2)
    stars, cads = take(len(late)), take(n_cad)
    before = [] if first else take(1 + len(lead))
    whi_out, wlo_out, loss_out = take(3)
    terms = take(len(lead))
    whole, lacc = refs
    width = whi_out.shape[0]
    good = quality[...].astype(F32)
    place_cads(whole, cads, cad_slot)
    rows = stars[0].shape[0] if late else 0
    right = product_right(of_slots(whole, star_slot, late, rows)) if late else None
    ghi, glo = two(of_slots(whole, star_slot, lead, rows) * (good * scale)) if lead else (None, None)
    gt = jnp.concatenate([glo.T, ghi.T, ghi.T], 0) if lead else None
    lacc[...] = jnp.zeros_like(lacc) if first else before[0][...]
    for start in range(0, width, SUB):
        at = pl.ds(start, SUB)
        residual = rest[pl.ds(offset + start, SUB), :]
        if late:
            s = jnp.concatenate([r[:, pl.ds((offset if r.shape[1] > width else 0) + start, SUB)] for r in stars], 0)
            residual = residual - mm(product_left(s), right, 0, 0)
        ratio = 1.0 + (residual * 0.5) ** 2
        whi, wlo = two(residual / ratio)
        whi_out[at, :], wlo_out[at, :] = whi, wlo
        if lead:
            term = mm(jnp.concatenate([whi, wlo, whi], 1), gt, 1, 0).T
            for k, ref in enumerate(terms):
                to = pl.ds(start if first else width + start, SUB)
                ref[:, to] = term[k * rows : (k + 1) * rows]
        q = SUB // 4
        prod = (ratio[:q] * ratio[q : 2 * q]) * (ratio[2 * q : 3 * q] * ratio[3 * q :])
        lacc[...] += jnp.sum(jnp.log(prod).reshape(q // 8, 8, -1), 0)
    if not last:
        loss_out[...] = lacc[...]
        return
    sums = lacc[...] * good
    lanes = sum(sums[:, c : c + 128] for c in range(0, sums.shape[1], 128))
    loss_out[...] = lanes
    for ref, half in zip(terms, before[1:], strict=True):
        ref[:, :width] = half[...]
        put_lanes(ref, lanes)


def put_lanes(ref, lanes):
    ref[:8, ref.shape[1] - 128 :] = lanes
    ref[8:, ref.shape[1] - 128 :] = jnp.zeros((ref.shape[0] - 8, 128), F32)


def sums_body(plan, *refs):
    scale, cad_scale, star_slot, cad_slot, slots, n_star, n_cad, chunks = plan
    refs = list(refs)
    take = lambda count: [refs.pop(0) for _ in range(count)]
    parts, loss, quality = take(2 * chunks), take(1)[0], take(1)[0]
    stars, halves, cads = take(n_star), take(chunks - 1), take(n_cad)
    outs = take(len(slots))
    keep, send, whole, acc = refs
    rows, crows = stars[0].shape[0], cads[0].shape[0]
    width = parts[0].shape[0]
    good = quality[...].astype(F32)
    place_cads(whole, cads, cad_slot)
    ghi, glo = two(of_slots(whole, star_slot, slots, rows) * (good * scale))
    gt = jnp.concatenate([glo.T, ghi.T, ghi.T], 0)
    acc[...] = jnp.zeros_like(acc)
    for c in range(chunks):
        pieces = list(stars)
        if c:
            pieces[n_star // 2] = halves[c - 1]
        for start in range(0, width, SUB):
            at = pl.ds(start, SUB)
            whi, wlo = parts[2 * c][at, :], parts[2 * c + 1][at, :]
            term = mm(jnp.concatenate([whi, wlo, whi], 1), gt, 1, 0).T
            for k, ref in enumerate(outs):
                ref[:, pl.ds(c * width + start, SUB)] = term[k * rows : (k + 1) * rows]
            s = jnp.concatenate([r[:, pl.ds((c * width if r.shape[1] > width else 0) + start, SUB)] for r in pieces], 0)
            shi, slo = two(s)
            acc[...] += mm(jnp.concatenate([slo, shi, shi], 1), jnp.concatenate([whi, wlo, whi], 0), 1, 0)
    if chunks > 1:
        for ref in outs:
            put_lanes(ref, loss[...])
    for k in range(n_star):
        whole[rank_rows(star_slot(k), rows), :] = acc[k * rows : (k + 1) * rows]
    mine = max(n_cad // 2, 1)
    for k in range(n_cad):
        ref, place = (keep, k) if k < mine else (send, k - mine)
        ref[pl.ds(place * crows, crows), :] = whole[rank_rows(cad_slot(k), crows), :] * (good * cad_scale)


def big_call(body_of, given, out_shape, scratch, macs):
    vmem = pl.BlockSpec(memory_space=pltpu.VMEM)
    return pl.pallas_call(
        body_of,
        in_specs=[vmem] * len(given),
        out_specs=[vmem] * len(out_shape),
        out_shape=out_shape,
        scratch_shapes=scratch,
        compiler_params=pltpu.CompilerParams(vmem_limit_bytes=24 << 20),
        cost_estimate=pl.CostEstimate(flops=2 * macs, bytes_accessed=1 << 20, transcendentals=0),
    )(*given)


def sds(*shape, kind=F32):
    return jax.ShapeDtypeStruct(shape, kind)


def early(light, stars, cads, star_slot, cad_slot, slots):
    count, nc = light.shape
    rank = cads[0].shape[0] * len(cads)
    plan = (star_slot, cad_slot, slots, len(cads))
    scratch = [pltpu.VMEM((rank, nc), F32)]
    return big_call(functools.partial(early_body, plan), [light] + stars + cads, [sds(count, nc)], scratch, 6 * count * nc * rank)[0]


def cells(rest, quality, stars, cads, before, scale, star_slot, cad_slot, late, lead, chunk, chunks):
    count, nc = rest.shape
    width = count // chunks
    rank = cads[0].shape[0] * len(cads)
    rows = stars[0].shape[0] if stars else 0
    first, last = chunk == 0, chunk == chunks - 1
    plan = (scale, star_slot, cad_slot, late, lead, len(cads), chunk * width, first, last)
    out = [sds(width, nc, kind=BF16)] * 2 + [sds(8, 128) if last else sds(8, nc)]
    out += [sds(rows, width if first else count + 128)] * len(lead)
    scratch = [pltpu.VMEM((rank, nc), F32), pltpu.VMEM((8, nc), F32)]
    return list(big_call(functools.partial(cells_body, plan), [rest, quality] + stars + cads + before, out, scratch, 4 * width * nc * rank))


def sums(parts, loss, quality, stars, halves, cads, scale, cad_scale, star_slot, cad_slot, slots):
    chunks, nc = len(parts) // 2, parts[0].shape[1]
    count = parts[0].shape[0] * chunks
    n_star, n_cad = len(stars), len(cads)
    rows, crows = stars[0].shape[0], cads[0].shape[0]
    rank = rows * n_star
    mine = max(n_cad // 2, 1)
    plan = (scale, cad_scale, star_slot, cad_slot, slots, n_star, n_cad, chunks)
    out = [sds(rows, count + (128 if chunks > 1 else 0))] * len(slots)
    out += [sds(crows * mine, nc), sds(crows * max(n_cad - mine, 1), nc)]
    scratch = [pltpu.VMEM((rank, nc), F32), pltpu.VMEM((rank, nc), F32)]
    given = parts + [loss, quality] + stars + halves + cads
    return list(big_call(functools.partial(sums_body, plan), given, out, scratch, 6 * count * nc * rank))


def small_call(body_of, given, shapes, limit=4):
    vmem = pl.BlockSpec(memory_space=pltpu.VMEM)
    return pl.pallas_call(
        body_of,
        in_specs=[vmem] * len(given),
        out_specs=[vmem] * len(shapes),
        out_shape=[jax.ShapeDtypeStruct(shape, F32) for shape in shapes],
        cost_estimate=pl.CostEstimate(flops=0, bytes_accessed=1 << 10, transcendentals=0),
        compiler_params=pltpu.CompilerParams(vmem_limit_bytes=limit << 20),
    )(*given)


def empty_body(*refs):
    pass


def hold(x, *after):
    anywhere = pl.BlockSpec(memory_space=pl.ANY)
    return pl.pallas_call(
        empty_body,
        in_specs=[anywhere] * (1 + len(after)),
        out_specs=anywhere,
        out_shape=jax.ShapeDtypeStruct(x.shape, x.dtype),
        input_output_aliases={0: 0},
        cost_estimate=pl.CostEstimate(flops=0, bytes_accessed=1 << 10, transcendentals=0),
        compiler_params=pltpu.CompilerParams(vmem_limit_bytes=1 << 20),
    )(x, *after)


def halve_body(keep, got, keep_out, send_out):
    rows = keep_out.shape[0]
    keep_out[...] = keep[:rows] + got[:rows]
    send_out[...] = keep[rows:] + got[rows:]


def halve(keep, got):
    shape = (keep.shape[0] // 2, keep.shape[1])
    return small_call(halve_body, [keep, got], [shape, shape])


def add_part_body(mine, got, out, part):
    out[...] = mine[...] + got[...]
    part[...] = out[:8, out.shape[1] - 128 :]


def add_part(mine, got):
    return small_call(add_part_body, [mine, got], [mine.shape, (8, 128)])


def loss_part_body(loss, near, beside, out):
    out[...] = loss[...] + near[...] + beside[:8, beside.shape[1] - 128 :]


def loss_part(loss, near, beside):
    return small_call(loss_part_body, [loss, near, beside], [(8, 128)])[0]


def last_stars_body(factor, mine, up, back, *refs):
    *losses, out, total = refs
    width = out.shape[1]
    out[...] = mine[:, :width] + up[:, :width] + back[:, :width]
    total[...] = jnp.sum(sum(ref[...] for ref in losses), keepdims=True) * factor


def last_stars(mine, up, back, losses, factor):
    rows, width = mine.shape
    shapes = [(rows, width - 128), (1, 1)]
    return small_call(functools.partial(last_stars_body, factor), [mine, up, back] + losses, shapes)


def ring_order(n):
    return list(range(0, n, 2)) + list(range(1, n, 2))[::-1]


def shift(x, core=0, places=1):
    m, n = lax.axis_size("star"), lax.axis_size("cad")
    order = ring_order(n)
    pairs = []
    for i in range(m):
        way = places if i % 2 == 0 else -places
        source, target = i ^ int(core < 0), i ^ int(core > 0)
        pairs += [(source * n + order[p], target * n + order[(p + way) % n]) for p in range(n)]
    return lax.ppermute(x, ("star", "cad"), pairs)


def swap(x, axis, bit):
    return lax.ppermute(x, axis, [(i, i ^ bit) for i in range(lax.axis_size(axis))])


def ring_program(light, quality, star_t, cad_t):
    n, m = lax.axis_size("cad"), lax.axis_size("star")
    count, nc = light.shape
    half = count // 2
    scale = -1.0 / float(nc * n) ** 0.5
    cad_scale = -1.0 / float(count * m) ** 0.5
    factor = 2.0 / (float(count * m) * float(nc * n))

    def star_slot(k):
        me = lax.axis_index("cad")
        place = jnp.where(me % 2 == 0, me // 2, n - 1 - me // 2)
        back = jnp.where(lax.axis_index("star") % 2 == 0, n - k, k)
        source = lax.rem(place + back, n)
        return jnp.where(source < n // 2, 2 * source, 2 * (n - 1 - source) + 1)

    def cad_slot(k):
        return jnp.bitwise_xor(lax.axis_index("star"), k)

    light = stage(light)[0]
    quality = quality.reshape(1, -1)

    with jax.named_scope("gather_cadence_factors"):
        cads = [cad_t] + [swap(cad_t, "star", bit) for bit in range(1, m)]

    far = n // 2
    pieces = [star_t] + [None] * (n - 1)
    with jax.named_scope("gather_star_factors"):
        beside = swap(star_t, "star", 1)
        for s in range(1, far):
            pieces[s] = shift(pieces[s - 1])
            if s == 1:
                beside = shift(beside)
                pieces[s], beside = hold(pieces[s], light), hold(beside, light)
            elif s < far - 1:
                beside = shift(beside)
                pieces[s] = hold(pieces[s], *cads[1:])
            else:
                beside = shift(beside, 1)
            pieces[n - s] = swap(beside, "star", 1) if s < far - 1 else beside
        far_a, far_b = shift(pieces[far - 1][:, :half]), shift(pieces[far - 1][:, half:])

    slots = [k for k in range(n) if k not in (far, far + 1)]
    rest = early(light, [pieces[k] for k in slots], cads, star_slot, cad_slot, slots)
    late, lead = [far, far + 1], [far, far - 1, far - 2]
    got_a = cells(rest, quality, [far_a, pieces[far + 1]], cads, [], scale, star_slot, cad_slot, late, lead, 0, 2)
    got_b = cells(rest, quality, [far_b, pieces[far + 1]], cads, got_a[2:], scale, star_slot, cad_slot, late, lead, 1, 2)
    loss = got_b[2]
    pieces[far] = far_a
    slots = [k for k in range(n) if k not in lead]
    second, third = swap(got_b[4], "star", 1), swap(got_b[5], "star", 1)
    loss = hold(loss, second)
    got = sums(got_a[:2] + got_b[:2], loss, quality, pieces, [far_b], cads, scale, cad_scale, star_slot, cad_slot, slots)
    terms = dict(zip(lead + slots, got_b[3:] + got[:-2], strict=True))
    keep, send = got[-2:]

    with jax.named_scope("scatter_star_gradient"):
        up, beside = shift(terms[far]), shift(second)
        up = shift(terms[far + 1] + up)
        message = third + beside
        keep, send = halve(keep, swap(hold(send, message), "star", 2))
        beside = shift(message)
        up = shift(hold(terms[far + 2] + up, message))
        cad_gradient = keep + swap(send, "star", 1)
        message = hold(swap(terms[1], "star", 1) + beside, keep)
        beside = shift(message)
        message, near = add_part(terms[far + 3], hold(up, message))
        near = shift(near)
        up = shift(message)
        back = swap(hold(beside, cad_gradient), "star", 1)
        part = loss_part(loss, near, beside)
        losses = [part] + [swap(part, "star", bit) for bit in range(1, m)]
        star_gradient, total = last_stars(terms[0], up, back, losses, factor)
    return (star_gradient.T, cad_gradient.T, total[0, 0])


def whole_program(light, quality, star_t, cad_t):
    n, m = lax.axis_size("cad"), lax.axis_size("star")
    count, nc = light.shape
    scale = -1.0 / float(nc * n) ** 0.5
    cad_scale = -1.0 / float(count * m) ** 0.5
    stars = [lax.all_gather(star_t, "cad", axis=0, tiled=True)]
    cads = [lax.all_gather(cad_t, "star", axis=0, tiled=True)]
    first = lambda k: 0
    light = early(light, stars, cads, first, first, [0])
    whi, wlo, loss = cells(light, quality.reshape(1, -1), [], cads, [], scale, first, first, [], [], 0, 1)
    parts = [whi, wlo]
    star, cad, _ = sums(parts, loss, quality.reshape(1, -1), stars, [], cads, scale, cad_scale, first, first, [0])
    star_gradient = lax.psum_scatter(star, "cad", scatter_dimension=0, tiled=True)
    cadence_gradient = lax.psum_scatter(cad, "star", scatter_dimension=0, tiled=True)
    loss = lax.psum(jnp.sum(loss), ("star", "cad")) * (2.0 / (float(count * m) * float(nc * n)))
    return (star_gradient.T, cadence_gradient.T, loss)


def on_device(light, quality, star_factors, cadence_factors):
    ring = lax.axis_size("cad") == 8 and lax.axis_size("star") == 4
    program = ring_program if ring else whole_program
    return program(light, quality, star_factors.T, cadence_factors.T)


def solution(mesh):
    in_specs = (P("star", "cad"), P("cad"), P("star", "cad"), P("cad", "star"))
    out_specs = (P("star", "cad"), P("cad", "star"), P())
    return jax.shard_map(
        on_device, mesh=mesh, in_specs=in_specs, out_specs=out_specs, check_vma=False
    )
```

```python
import functools

import jax
import jax.numpy as jnp
from jax import lax
from jax.experimental import pallas as pl
from jax.experimental.pallas import tpu as pltpu
from jax.sharding import PartitionSpec as P

F32 = jnp.float32
BF16 = jnp.bfloat16
SUB = 512


def two(x):
    hi = x.astype(BF16)
    return hi, (x - hi.astype(F32)).astype(BF16)


def three(x):
    hi = x.astype(BF16)
    rest = x - hi.astype(F32)
    mid = rest.astype(BF16)
    return hi, mid, (rest - mid.astype(F32)).astype(BF16)


def mm(a, b, ca, cb):
    return lax.dot_general(a, b, (((ca,), (cb,)), ((), ())), preferred_element_type=F32)


def rank_rows(k, rows):
    return pl.ds(pl.multiple_of(k * rows, rows), rows)


def stage_body(*refs):
    count = len(refs) // 2
    sem = refs[-1]
    copies = [pltpu.make_async_copy(refs[i], refs[count + i], sem.at[i]) for i in range(count)]
    for copy in copies:
        copy.start()
    for copy in copies:
        copy.wait()


def stage(*given):
    return pl.pallas_call(
        stage_body,
        in_specs=[pl.BlockSpec(memory_space=pl.ANY)] * len(given),
        out_specs=[pl.BlockSpec(memory_space=pltpu.VMEM)] * len(given),
        out_shape=[jax.ShapeDtypeStruct(x.shape, x.dtype) for x in given],
        scratch_shapes=[pltpu.SemaphoreType.DMA((len(given),))],
        cost_estimate=pl.CostEstimate(flops=0, bytes_accessed=1 << 10, transcendentals=0),
        compiler_params=pltpu.CompilerParams(vmem_limit_bytes=16 << 20),
    )(*given)


def place_cads(whole, cads, cad_slot):
    rows = cads[0].shape[0]
    for k, ref in enumerate(cads):
        whole[rank_rows(cad_slot(k), rows), :] = ref[...]


def of_slots(whole, star_slot, slots, rows):
    return jnp.concatenate([whole[rank_rows(star_slot(k), rows), :] for k in slots], 0)


def columns(refs, start, size):
    return jnp.concatenate([ref[:, pl.ds(start, size)] for ref in refs], 0)


def product_left(s):
    hi, mid, lo = three(s)
    return jnp.concatenate([hi, lo, mid, mid, hi, hi], 0)


def product_right(c):
    hi, mid, lo = three(c)
    return jnp.concatenate([lo, hi, hi, mid, hi, mid], 0)


def early_body(plan, *refs):
    star_slot, cad_slot, slots, n_cad = plan
    light, refs = refs[0], refs[1:]
    stars, cads = refs[: len(slots)], refs[len(slots) : len(slots) + n_cad]
    out, whole = refs[-2:]
    rows = stars[0].shape[0]
    place_cads(whole, cads, cad_slot)
    pad = -rows * len(slots) % 128
    block = of_slots(whole, star_slot, slots, rows)
    if pad:
        block = jnp.concatenate([block, jnp.zeros((pad, block.shape[1]), F32)], 0)
    right = product_right(block)
    for start in range(0, light.shape[0], SUB):
        s = columns(stars, start, SUB)
        if pad:
            s = jnp.concatenate([s, jnp.zeros((pad, SUB), F32)], 0)
        hi, mid, lo = three(s.T)
        left = jnp.concatenate([hi, lo, mid, mid, hi, hi], 1)
        at = pl.ds(start, SUB)
        out[at, :] = light[at, :] - mm(left, right, 1, 0)


def cells_body(plan, *refs):
    scale, star_slot, cad_slot, late, lead, n_cad, offset, first, last = plan
    refs = list(refs)
    take = lambda count: [refs.pop(0) for _ in range(count)]
    rest, quality = take(2)
    stars, cads = take(len(late)), take(n_cad)
    before = [] if first else take(1 + len(lead))
    whi_out, wlo_out, loss_out = take(3)
    terms = take(len(lead))
    whole, lacc = refs
    width = whi_out.shape[0]
    good = quality[...].astype(F32)
    place_cads(whole, cads, cad_slot)
    rows = stars[0].shape[0] if late else 0
    right = product_right(of_slots(whole, star_slot, late, rows)) if late else None
    ghi, glo = two(of_slots(whole, star_slot, lead, rows) * (good * scale)) if lead else (None, None)
    gt = jnp.concatenate([glo.T, ghi.T, ghi.T], 0) if lead else None
    lacc[...] = jnp.zeros_like(lacc) if first else before[0][...]
    for start in range(0, width, SUB):
        at = pl.ds(start, SUB)
        residual = rest[pl.ds(offset + start, SUB), :]
        if late:
            s = jnp.concatenate([r[:, pl.ds((offset if r.shape[1] > width else 0) + start, SUB)] for r in stars], 0)
            residual = residual - mm(product_left(s), right, 0, 0)
        ratio = 1.0 + (residual * 0.5) ** 2
        whi, wlo = two(residual / ratio)
        whi_out[at, :], wlo_out[at, :] = whi, wlo
        if lead:
            term = mm(jnp.concatenate([whi, wlo, whi], 1), gt, 1, 0).T
            for k, ref in enumerate(terms):
                to = pl.ds(start if first else width + start, SUB)
                ref[:, to] = term[k * rows : (k + 1) * rows]
        q = SUB // 4
        prod = (ratio[:q] * ratio[q : 2 * q]) * (ratio[2 * q : 3 * q] * ratio[3 * q :])
        lacc[...] += jnp.sum(jnp.log(prod).reshape(q // 8, 8, -1), 0)
    if not last:
        loss_out[...] = lacc[...]
        return
    sums = lacc[...] * good
    lanes = sum(sums[:, c : c + 128] for c in range(0, sums.shape[1], 128))
    loss_out[...] = lanes
    for ref, half in zip(terms, before[1:], strict=True):
        ref[:, :width] = half[...]
        put_lanes(ref, lanes)


def put_lanes(ref, lanes):
    ref[:8, ref.shape[1] - 128 :] = lanes
    ref[8:, ref.shape[1] - 128 :] = jnp.zeros((ref.shape[0] - 8, 128), F32)


def sums_body(plan, *refs):
    scale, cad_scale, star_slot, cad_slot, slots, n_star, n_cad, chunks = plan
    refs = list(refs)
    take = lambda count: [refs.pop(0) for _ in range(count)]
    parts, loss, quality = take(2 * chunks), take(1)[0], take(1)[0]
    stars, halves, cads = take(n_star), take(chunks - 1), take(n_cad)
    outs = take(len(slots))
    keep, send, whole, acc = refs
    rows, crows = stars[0].shape[0], cads[0].shape[0]
    width = parts[0].shape[0]
    good = quality[...].astype(F32)
    place_cads(whole, cads, cad_slot)
    ghi, glo = two(of_slots(whole, star_slot, slots, rows) * (good * scale))
    gt = jnp.concatenate([glo.T, ghi.T, ghi.T], 0)
    acc[...] = jnp.zeros_like(acc)
    for c in range(chunks):
        pieces = list(stars)
        if c:
            pieces[n_star // 2] = halves[c - 1]
        for start in range(0, width, SUB):
            at = pl.ds(start, SUB)
            whi, wlo = parts[2 * c][at, :], parts[2 * c + 1][at, :]
            term = mm(jnp.concatenate([whi, wlo, whi], 1), gt, 1, 0).T
            for k, ref in enumerate(outs):
                ref[:, pl.ds(c * width + start, SUB)] = term[k * rows : (k + 1) * rows]
            s = jnp.concatenate([r[:, pl.ds((c * width if r.shape[1] > width else 0) + start, SUB)] for r in pieces], 0)
            shi, slo = two(s)
            acc[...] += mm(jnp.concatenate([slo, shi, shi], 1), jnp.concatenate([whi, wlo, whi], 0), 1, 0)
    if chunks > 1:
        for ref in outs:
            put_lanes(ref, loss[...])
    for k in range(n_star):
        whole[rank_rows(star_slot(k), rows), :] = acc[k * rows : (k + 1) * rows]
    mine = max(n_cad // 2, 1)
    for k in range(n_cad):
        ref, place = (keep, k) if k < mine else (send, k - mine)
        ref[pl.ds(place * crows, crows), :] = whole[rank_rows(cad_slot(k), crows), :] * (good * cad_scale)


def big_call(body_of, given, out_shape, scratch, macs):
    vmem = pl.BlockSpec(memory_space=pltpu.VMEM)
    return pl.pallas_call(
        body_of,
        in_specs=[vmem] * len(given),
        out_specs=[vmem] * len(out_shape),
        out_shape=out_shape,
        scratch_shapes=scratch,
        compiler_params=pltpu.CompilerParams(vmem_limit_bytes=24 << 20),
        cost_estimate=pl.CostEstimate(flops=2 * macs, bytes_accessed=1 << 20, transcendentals=0),
    )(*given)


def sds(*shape, kind=F32):
    return jax.ShapeDtypeStruct(shape, kind)


def early(light, stars, cads, star_slot, cad_slot, slots):
    count, nc = light.shape
    rank = cads[0].shape[0] * len(cads)
    plan = (star_slot, cad_slot, slots, len(cads))
    scratch = [pltpu.VMEM((rank, nc), F32)]
    return big_call(functools.partial(early_body, plan), [light] + stars + cads, [sds(count, nc)], scratch, 6 * count * nc * rank)[0]


def cells(rest, quality, stars, cads, before, scale, star_slot, cad_slot, late, lead, chunk, chunks):
    count, nc = rest.shape
    width = count // chunks
    rank = cads[0].shape[0] * len(cads)
    rows = stars[0].shape[0] if stars else 0
    first, last = chunk == 0, chunk == chunks - 1
    plan = (scale, star_slot, cad_slot, late, lead, len(cads), chunk * width, first, last)
    out = [sds(width, nc, kind=BF16)] * 2 + [sds(8, 128) if last else sds(8, nc)]
    out += [sds(rows, width if first else count + 128)] * len(lead)
    scratch = [pltpu.VMEM((rank, nc), F32), pltpu.VMEM((8, nc), F32)]
    return list(big_call(functools.partial(cells_body, plan), [rest, quality] + stars + cads + before, out, scratch, 4 * width * nc * rank))


def sums(parts, loss, quality, stars, halves, cads, scale, cad_scale, star_slot, cad_slot, slots):
    chunks, nc = len(parts) // 2, parts[0].shape[1]
    count = parts[0].shape[0] * chunks
    n_star, n_cad = len(stars), len(cads)
    rows, crows = stars[0].shape[0], cads[0].shape[0]
    rank = rows * n_star
    mine = max(n_cad // 2, 1)
    plan = (scale, cad_scale, star_slot, cad_slot, slots, n_star, n_cad, chunks)
    out = [sds(rows, count + (128 if chunks > 1 else 0))] * len(slots)
    out += [sds(crows * mine, nc), sds(crows * max(n_cad - mine, 1), nc)]
    scratch = [pltpu.VMEM((rank, nc), F32), pltpu.VMEM((rank, nc), F32)]
    given = parts + [loss, quality] + stars + halves + cads
    return list(big_call(functools.partial(sums_body, plan), given, out, scratch, 6 * count * nc * rank))


def small_call(body_of, given, shapes, weight=0):
    vmem = pl.BlockSpec(memory_space=pltpu.VMEM)
    return pl.pallas_call(
        body_of,
        in_specs=[vmem] * len(given),
        out_specs=[vmem] * len(shapes),
        out_shape=[jax.ShapeDtypeStruct(shape, F32) for shape in shapes],
        cost_estimate=pl.CostEstimate(flops=weight, bytes_accessed=1 << 10, transcendentals=0),
        compiler_params=pltpu.CompilerParams(vmem_limit_bytes=4 << 20),
    )(*given)


def empty_body(*refs):
    pass


def hold(x, *after):
    anywhere = pl.BlockSpec(memory_space=pl.ANY)
    return pl.pallas_call(
        empty_body,
        in_specs=[anywhere] * (1 + len(after)),
        out_specs=anywhere,
        out_shape=jax.ShapeDtypeStruct(x.shape, x.dtype),
        input_output_aliases={0: 0},
        cost_estimate=pl.CostEstimate(flops=0, bytes_accessed=1 << 10, transcendentals=0),
        compiler_params=pltpu.CompilerParams(vmem_limit_bytes=1 << 20),
    )(x, *after)


def halve_body(keep, got, keep_out, send_out):
    rows = keep_out.shape[0]
    keep_out[...] = keep[:rows] + got[:rows]
    send_out[...] = keep[rows:] + got[rows:]


def halve(keep, got):
    shape = (keep.shape[0] // 2, keep.shape[1])
    return small_call(halve_body, [keep, got], [shape, shape])


def add_part_body(mine, got, out, part):
    out[...] = mine[...] + got[...]
    part[...] = out[:8, out.shape[1] - 128 :]


def add_part(mine, got):
    return small_call(add_part_body, [mine, got], [mine.shape, (8, 128)])


def loss_part_body(loss, near, beside, out):
    out[...] = loss[...] + near[...] + beside[:8, beside.shape[1] - 128 :]


def loss_part(loss, near, beside):
    return small_call(loss_part_body, [loss, near, beside], [(8, 128)], weight=3 * 10**9)[0]


def add_losses_body(*refs):
    refs[-1][...] = sum(ref[...] for ref in refs[:-1])


def add_losses(losses):
    return small_call(add_losses_body, losses, [(8, 128)])[0]


def last_sums_body(factor, mine, up, back, keep, got, *refs):
    *losses, out, cad_out, total = refs
    width = out.shape[1]
    out[...] = mine[:, :width] + up[:, :width] + back[:, :width]
    cad_out[...] = keep[...] + got[...]
    total[...] = jnp.sum(sum(ref[...] for ref in losses), keepdims=True) * factor


def last_sums(mine, up, back, kept, losses, factor):
    rows, width = mine.shape
    shapes = [(rows, width - 128), kept[0].shape, (1, 1)]
    return small_call(functools.partial(last_sums_body, factor), [mine, up, back] + kept + losses, shapes)


def ring_order(n):
    return list(range(0, n, 2)) + list(range(1, n, 2))[::-1]


def shift(x, core=0, places=1):
    m, n = lax.axis_size("star"), lax.axis_size("cad")
    order = ring_order(n)
    pairs = []
    for i in range(m):
        way = places if i % 2 == 0 else -places
        source, target = i ^ int(core < 0), i ^ int(core > 0)
        pairs += [(source * n + order[p], target * n + order[(p + way) % n]) for p in range(n)]
    return lax.ppermute(x, ("star", "cad"), pairs)


def swap(x, axis, bit):
    return lax.ppermute(x, axis, [(i, i ^ bit) for i in range(lax.axis_size(axis))])


def ring_program(light, quality, star_t, cad_t):
    n, m = lax.axis_size("cad"), lax.axis_size("star")
    count, nc = light.shape
    half = count // 2
    scale = -1.0 / float(nc * n) ** 0.5
    cad_scale = -1.0 / float(count * m) ** 0.5
    factor = 2.0 / (float(count * m) * float(nc * n))

    def star_slot(k):
        me = lax.axis_index("cad")
        place = jnp.where(me % 2 == 0, me // 2, n - 1 - me // 2)
        back = jnp.where(lax.axis_index("star") % 2 == 0, n - k, k)
        source = lax.rem(place + back, n)
        return jnp.where(source < n // 2, 2 * source, 2 * (n - 1 - source) + 1)

    def cad_slot(k):
        return jnp.bitwise_xor(lax.axis_index("star"), k)

    light = stage(light)[0]
    quality = quality.reshape(1, -1)

    with jax.named_scope("gather_cadence_factors"):
        cads = [cad_t] + [swap(cad_t, "star", bit) for bit in range(1, m)]

    far = n // 2
    pieces = [star_t] + [None] * (n - 1)
    with jax.named_scope("gather_star_factors"):
        beside = swap(star_t, "star", 1)
        for s in range(1, far):
            pieces[s] = shift(pieces[s - 1])
            if s == 1:
                beside = shift(beside)
                pieces[s], beside = hold(pieces[s], light), hold(beside, light)
            elif s < far - 1:
                beside = shift(beside)
                pieces[s] = hold(pieces[s], *cads[1:])
            else:
                beside = shift(beside, 1)
            pieces[n - s] = swap(beside, "star", 1) if s < far - 1 else beside
        far_a, far_b = shift(pieces[far - 1][:, :half]), shift(pieces[far - 1][:, half:])

    slots = [k for k in range(n) if k not in (far, far + 1)]
    rest = early(light, [pieces[k] for k in slots], cads, star_slot, cad_slot, slots)
    late, lead = [far, far + 1], [far, far - 1, far - 2]
    got_a = cells(rest, quality, [far_a, pieces[far + 1]], cads, [], scale, star_slot, cad_slot, late, lead, 0, 2)
    got_b = cells(rest, quality, [far_b, pieces[far + 1]], cads, got_a[2:], scale, star_slot, cad_slot, late, lead, 1, 2)
    loss = got_b[2]
    pieces[far] = far_a
    slots = [k for k in range(n) if k not in lead]
    second, third = swap(got_b[4], "star", 1), swap(got_b[5], "star", 1)
    loss = hold(loss, second)
    got = sums(got_a[:2] + got_b[:2], loss, quality, pieces, [far_b], cads, scale, cad_scale, star_slot, cad_slot, slots)
    terms = dict(zip(lead + slots, got_b[3:] + got[:-2], strict=True))
    keep, send = got[-2:]

    with jax.named_scope("scatter_star_gradient"):
        up, beside = shift(terms[far]), shift(second)
        up = shift(terms[far + 1] + up)
        message = third + beside
        keep, send = halve(keep, swap(hold(send, message), "star", 2))
        beside = shift(message)
        up = shift(hold(terms[far + 2] + up, message))
        message = hold(swap(terms[1], "star", 1) + beside, keep)
        beside = shift(message, 1)
        message, near = add_part(terms[far + 3], hold(up, message))
        near = shift(near)
        up = shift(message)
        part = loss_part(loss, near, beside)
        part = add_losses([part, swap(part, "star", 1)])
        losses = [part, swap(part, "star", 2)]
        kept = [keep, swap(hold(send, beside), "star", 1)]
        star_gradient, cad_gradient, total = last_sums(terms[0], up, beside, kept, losses, factor)
    return (star_gradient.T, cad_gradient.T, total[0, 0])


def whole_program(light, quality, star_t, cad_t):
    n, m = lax.axis_size("cad"), lax.axis_size("star")
    count, nc = light.shape
    scale = -1.0 / float(nc * n) ** 0.5
    cad_scale = -1.0 / float(count * m) ** 0.5
    stars = [lax.all_gather(star_t, "cad", axis=0, tiled=True)]
    cads = [lax.all_gather(cad_t, "star", axis=0, tiled=True)]
    first = lambda k: 0
    light = early(light, stars, cads, first, first, [0])
    whi, wlo, loss = cells(light, quality.reshape(1, -1), [], cads, [], scale, first, first, [], [], 0, 1)
    parts = [whi, wlo]
    star, cad, _ = sums(parts, loss, quality.reshape(1, -1), stars, [], cads, scale, cad_scale, first, first, [0])
    star_gradient = lax.psum_scatter(star, "cad", scatter_dimension=0, tiled=True)
    cadence_gradient = lax.psum_scatter(cad, "star", scatter_dimension=0, tiled=True)
    loss = lax.psum(jnp.sum(loss), ("star", "cad")) * (2.0 / (float(count * m) * float(nc * n)))
    return (star_gradient.T, cadence_gradient.T, loss)


def on_device(light, quality, star_factors, cadence_factors):
    ring = lax.axis_size("cad") == 8 and lax.axis_size("star") == 4
    program = ring_program if ring else whole_program
    return program(light, quality, star_factors.T, cadence_factors.T)


def solution(mesh):
    in_specs = (P("star", "cad"), P("cad"), P("star", "cad"), P("cad", "star"))
    out_specs = (P("star", "cad"), P("cad", "star"), P())
    return jax.shard_map(
        on_device, mesh=mesh, in_specs=in_specs, out_specs=out_specs, check_vma=False
    )
```

```python
import functools

import jax
import jax.numpy as jnp
from jax import lax
from jax.experimental import pallas as pl
from jax.experimental.pallas import tpu as pltpu
from jax.sharding import PartitionSpec as P

F32 = jnp.float32
BF16 = jnp.bfloat16
SUB = 512


def two(x):
    hi = x.astype(BF16)
    return hi, (x - hi.astype(F32)).astype(BF16)


def three(x):
    hi = x.astype(BF16)
    rest = x - hi.astype(F32)
    mid = rest.astype(BF16)
    return hi, mid, (rest - mid.astype(F32)).astype(BF16)


def mm(a, b, ca, cb):
    return lax.dot_general(a, b, (((ca,), (cb,)), ((), ())), preferred_element_type=F32)


def rank_rows(k, rows):
    return pl.ds(pl.multiple_of(k * rows, rows), rows)


def stage_body(*refs):
    count = len(refs) // 2
    sem = refs[-1]
    copies = [pltpu.make_async_copy(refs[i], refs[count + i], sem.at[i]) for i in range(count)]
    for copy in copies:
        copy.start()
    for copy in copies:
        copy.wait()


def stage(*given):
    return pl.pallas_call(
        stage_body,
        in_specs=[pl.BlockSpec(memory_space=pl.ANY)] * len(given),
        out_specs=[pl.BlockSpec(memory_space=pltpu.VMEM)] * len(given),
        out_shape=[jax.ShapeDtypeStruct(x.shape, x.dtype) for x in given],
        scratch_shapes=[pltpu.SemaphoreType.DMA((len(given),))],
        cost_estimate=pl.CostEstimate(flops=0, bytes_accessed=1 << 10, transcendentals=0),
        compiler_params=pltpu.CompilerParams(vmem_limit_bytes=16 << 20),
    )(*given)


def place_cads(whole, cads, cad_slot):
    rows = cads[0].shape[0]
    for k, ref in enumerate(cads):
        whole[rank_rows(cad_slot(k), rows), :] = ref[...]


def of_slots(whole, star_slot, slots, rows):
    return jnp.concatenate([whole[rank_rows(star_slot(k), rows), :] for k in slots], 0)


def columns(refs, start, size):
    return jnp.concatenate([ref[:, pl.ds(start, size)] for ref in refs], 0)


def product_left(s):
    hi, mid, lo = three(s)
    return jnp.concatenate([hi, lo, mid, mid, hi, hi], 0)


def product_right(c):
    hi, mid, lo = three(c)
    return jnp.concatenate([lo, hi, hi, mid, hi, mid], 0)


def early_body(plan, *refs):
    star_slot, cad_slot, slots, n_cad = plan
    light, refs = refs[0], refs[1:]
    stars, cads = refs[: len(slots)], refs[len(slots) : len(slots) + n_cad]
    out, whole = refs[-2:]
    rows = stars[0].shape[0]
    place_cads(whole, cads, cad_slot)
    pad = -rows * len(slots) % 128
    block = of_slots(whole, star_slot, slots, rows)
    if pad:
        block = jnp.concatenate([block, jnp.zeros((pad, block.shape[1]), F32)], 0)
    right = product_right(block)
    for start in range(0, light.shape[0], SUB):
        s = columns(stars, start, SUB)
        if pad:
            s = jnp.concatenate([s, jnp.zeros((pad, SUB), F32)], 0)
        hi, mid, lo = three(s.T)
        left = jnp.concatenate([hi, lo, mid, mid, hi, hi], 1)
        at = pl.ds(start, SUB)
        out[at, :] = light[at, :] - mm(left, right, 1, 0)


def cells_body(plan, *refs):
    scale, star_slot, cad_slot, late, lead, n_cad, offset, first, last = plan
    refs = list(refs)
    take = lambda count: [refs.pop(0) for _ in range(count)]
    rest, quality = take(2)
    stars, cads = take(len(late)), take(n_cad)
    before = [] if first else take(1 + len(lead))
    whi_out, wlo_out, loss_out = take(3)
    terms = take(len(lead))
    whole, lacc = refs
    width = whi_out.shape[0]
    good = quality[...].astype(F32)
    place_cads(whole, cads, cad_slot)
    rows = stars[0].shape[0] if late else 0
    right = product_right(of_slots(whole, star_slot, late, rows)) if late else None
    ghi, glo = two(of_slots(whole, star_slot, lead, rows) * (good * scale)) if lead else (None, None)
    gt = jnp.concatenate([glo.T, ghi.T, ghi.T], 0) if lead else None
    lacc[...] = jnp.zeros_like(lacc) if first else before[0][...]
    for start in range(0, width, SUB):
        at = pl.ds(start, SUB)
        residual = rest[pl.ds(offset + start, SUB), :]
        if late:
            s = jnp.concatenate([r[:, pl.ds((offset if r.shape[1] > width else 0) + start, SUB)] for r in stars], 0)
            residual = residual - mm(product_left(s), right, 0, 0)
        ratio = 1.0 + (residual * 0.5) ** 2
        whi, wlo = two(residual / ratio)
        whi_out[at, :], wlo_out[at, :] = whi, wlo
        if lead:
            term = mm(jnp.concatenate([whi, wlo, whi], 1), gt, 1, 0).T
            for k, ref in enumerate(terms):
                to = pl.ds(start if first else width + start, SUB)
                ref[:, to] = term[k * rows : (k + 1) * rows]
        q = SUB // 4
        prod = (ratio[:q] * ratio[q : 2 * q]) * (ratio[2 * q : 3 * q] * ratio[3 * q :])
        lacc[...] += jnp.sum(jnp.log(prod).reshape(q // 8, 8, -1), 0)
    if not last:
        loss_out[...] = lacc[...]
        return
    sums = lacc[...] * good
    lanes = sum(sums[:, c : c + 128] for c in range(0, sums.shape[1], 128))
    loss_out[...] = lanes
    for ref, half in zip(terms, before[1:], strict=True):
        ref[:, :width] = half[...]
        put_lanes(ref, lanes)


def put_lanes(ref, lanes):
    ref[:8, ref.shape[1] - 128 :] = lanes
    ref[8:, ref.shape[1] - 128 :] = jnp.zeros((ref.shape[0] - 8, 128), F32)


def sums_body(plan, *refs):
    scale, cad_scale, star_slot, cad_slot, slots, n_star, n_cad, chunks = plan
    refs = list(refs)
    take = lambda count: [refs.pop(0) for _ in range(count)]
    parts, loss, quality = take(2 * chunks), take(1)[0], take(1)[0]
    stars, halves, cads = take(n_star), take(chunks - 1), take(n_cad)
    outs = take(len(slots))
    keep, send, whole, acc = refs
    rows, crows = stars[0].shape[0], cads[0].shape[0]
    width = parts[0].shape[0]
    good = quality[...].astype(F32)
    place_cads(whole, cads, cad_slot)
    ghi, glo = two(of_slots(whole, star_slot, slots, rows) * (good * scale))
    gt = jnp.concatenate([glo.T, ghi.T, ghi.T], 0)
    acc[...] = jnp.zeros_like(acc)
    for c in range(chunks):
        pieces = list(stars)
        if c:
            pieces[n_star // 2] = halves[c - 1]
        for start in range(0, width, SUB):
            at = pl.ds(start, SUB)
            whi, wlo = parts[2 * c][at, :], parts[2 * c + 1][at, :]
            term = mm(jnp.concatenate([whi, wlo, whi], 1), gt, 1, 0).T
            for k, ref in enumerate(outs):
                ref[:, pl.ds(c * width + start, SUB)] = term[k * rows : (k + 1) * rows]
            s = jnp.concatenate([r[:, pl.ds((c * width if r.shape[1] > width else 0) + start, SUB)] for r in pieces], 0)
            shi, slo = two(s)
            acc[...] += mm(jnp.concatenate([slo, shi, shi], 1), jnp.concatenate([whi, wlo, whi], 0), 1, 0)
    if chunks > 1:
        for ref in outs:
            put_lanes(ref, loss[...])
    for k in range(n_star):
        whole[rank_rows(star_slot(k), rows), :] = acc[k * rows : (k + 1) * rows]
    mine = max(n_cad // 2, 1)
    for k in range(n_cad):
        ref, place = (keep, k) if k < mine else (send, k - mine)
        ref[pl.ds(place * crows, crows), :] = whole[rank_rows(cad_slot(k), crows), :] * (good * cad_scale)


def big_call(body_of, given, out_shape, scratch, macs):
    vmem = pl.BlockSpec(memory_space=pltpu.VMEM)
    return pl.pallas_call(
        body_of,
        in_specs=[vmem] * len(given),
        out_specs=[vmem] * len(out_shape),
        out_shape=out_shape,
        scratch_shapes=scratch,
        compiler_params=pltpu.CompilerParams(vmem_limit_bytes=24 << 20),
        cost_estimate=pl.CostEstimate(flops=2 * macs, bytes_accessed=1 << 20, transcendentals=0),
    )(*given)


def sds(*shape, kind=F32):
    return jax.ShapeDtypeStruct(shape, kind)


def early(light, stars, cads, star_slot, cad_slot, slots):
    count, nc = light.shape
    rank = cads[0].shape[0] * len(cads)
    plan = (star_slot, cad_slot, slots, len(cads))
    scratch = [pltpu.VMEM((rank, nc), F32)]
    return big_call(functools.partial(early_body, plan), [light] + stars + cads, [sds(count, nc)], scratch, 6 * count * nc * rank)[0]


def cells(rest, quality, stars, cads, before, scale, star_slot, cad_slot, late, lead, chunk, chunks):
    count, nc = rest.shape
    width = count // chunks
    rank = cads[0].shape[0] * len(cads)
    rows = stars[0].shape[0] if stars else 0
    first, last = chunk == 0, chunk == chunks - 1
    plan = (scale, star_slot, cad_slot, late, lead, len(cads), chunk * width, first, last)
    out = [sds(width, nc, kind=BF16)] * 2 + [sds(8, 128) if last else sds(8, nc)]
    out += [sds(rows, width if first else count + 128)] * len(lead)
    scratch = [pltpu.VMEM((rank, nc), F32), pltpu.VMEM((8, nc), F32)]
    return list(big_call(functools.partial(cells_body, plan), [rest, quality] + stars + cads + before, out, scratch, 4 * width * nc * rank))


def sums(parts, loss, quality, stars, halves, cads, scale, cad_scale, star_slot, cad_slot, slots):
    chunks, nc = len(parts) // 2, parts[0].shape[1]
    count = parts[0].shape[0] * chunks
    n_star, n_cad = len(stars), len(cads)
    rows, crows = stars[0].shape[0], cads[0].shape[0]
    rank = rows * n_star
    mine = max(n_cad // 2, 1)
    plan = (scale, cad_scale, star_slot, cad_slot, slots, n_star, n_cad, chunks)
    out = [sds(rows, count + (128 if chunks > 1 else 0))] * len(slots)
    out += [sds(crows * mine, nc), sds(crows * max(n_cad - mine, 1), nc)]
    scratch = [pltpu.VMEM((rank, nc), F32), pltpu.VMEM((rank, nc), F32)]
    given = parts + [loss, quality] + stars + halves + cads
    return list(big_call(functools.partial(sums_body, plan), given, out, scratch, 6 * count * nc * rank))


def small_call(body_of, given, shapes, weight=0):
    vmem = pl.BlockSpec(memory_space=pltpu.VMEM)
    return pl.pallas_call(
        body_of,
        in_specs=[vmem] * len(given),
        out_specs=[vmem] * len(shapes),
        out_shape=[jax.ShapeDtypeStruct(shape, F32) for shape in shapes],
        cost_estimate=pl.CostEstimate(flops=weight, bytes_accessed=1 << 10, transcendentals=0),
        compiler_params=pltpu.CompilerParams(vmem_limit_bytes=4 << 20),
    )(*given)


def empty_body(*refs):
    pass


def hold(x, *after):
    anywhere = pl.BlockSpec(memory_space=pl.ANY)
    return pl.pallas_call(
        empty_body,
        in_specs=[anywhere] * (1 + len(after)),
        out_specs=anywhere,
        out_shape=jax.ShapeDtypeStruct(x.shape, x.dtype),
        input_output_aliases={0: 0},
        cost_estimate=pl.CostEstimate(flops=0, bytes_accessed=1 << 10, transcendentals=0),
        compiler_params=pltpu.CompilerParams(vmem_limit_bytes=1 << 20),
    )(x, *after)


def halve_body(keep, got, keep_out, send_out):
    rows = keep_out.shape[0]
    keep_out[...] = keep[:rows] + got[:rows]
    send_out[...] = keep[rows:] + got[rows:]


def halve(keep, got):
    shape = (keep.shape[0] // 2, keep.shape[1])
    return small_call(halve_body, [keep, got], [shape, shape])


def add_part_body(mine, got, out, part):
    width = out.shape[1]
    out[...] = mine[:, :width] + got[:, :width]
    part[...] = mine[:8, width:] + got[:8, width:]


def add_part(mine, got):
    return small_call(add_part_body, [mine, got], [(mine.shape[0], mine.shape[1] - 128), (8, 128)])


def loss_part_body(loss, near, beside, out):
    out[...] = loss[...] + near[...] + beside[:8, beside.shape[1] - 128 :]


def loss_part(loss, near, beside):
    return small_call(loss_part_body, [loss, near, beside], [(8, 128)], weight=3 * 10**9)[0]


def add_losses_body(*refs):
    refs[-1][...] = sum(ref[...] for ref in refs[:-1])


def add_losses(losses):
    return small_call(add_losses_body, losses, [(8, 128)])[0]


def last_sums_body(factor, mine, up, back, keep, got, *refs):
    *losses, out, cad_out, total = refs
    width = out.shape[1]
    out[...] = mine[:, :width] + up[:, :width] + back[:, :width]
    cad_out[...] = keep[...] + got[...]
    total[...] = jnp.sum(sum(ref[...] for ref in losses), keepdims=True) * factor


def last_sums(mine, up, back, kept, losses, factor):
    rows, width = mine.shape
    shapes = [(rows, width - 128), kept[0].shape, (1, 1)]
    return small_call(functools.partial(last_sums_body, factor), [mine, up, back] + kept + losses, shapes)


def ring_order(n):
    return list(range(0, n, 2)) + list(range(1, n, 2))[::-1]


def shift(x, core=0, places=1):
    m, n = lax.axis_size("star"), lax.axis_size("cad")
    order = ring_order(n)
    pairs = []
    for i in range(m):
        way = places if i % 2 == 0 else -places
        source, target = i ^ int(core < 0), i ^ int(core > 0)
        pairs += [(source * n + order[p], target * n + order[(p + way) % n]) for p in range(n)]
    return lax.ppermute(x, ("star", "cad"), pairs)


def swap(x, axis, bit):
    return lax.ppermute(x, axis, [(i, i ^ bit) for i in range(lax.axis_size(axis))])


def ring_program(light, quality, star_t, cad_t):
    n, m = lax.axis_size("cad"), lax.axis_size("star")
    count, nc = light.shape
    half = count // 2
    scale = -1.0 / float(nc * n) ** 0.5
    cad_scale = -1.0 / float(count * m) ** 0.5
    factor = 2.0 / (float(count * m) * float(nc * n))

    def star_slot(k):
        me = lax.axis_index("cad")
        place = jnp.where(me % 2 == 0, me // 2, n - 1 - me // 2)
        back = jnp.where(lax.axis_index("star") % 2 == 0, n - k, k)
        source = lax.rem(place + back, n)
        return jnp.where(source < n // 2, 2 * source, 2 * (n - 1 - source) + 1)

    def cad_slot(k):
        return jnp.bitwise_xor(lax.axis_index("star"), k)

    light = stage(light)[0]
    quality = quality.reshape(1, -1)

    with jax.named_scope("gather_cadence_factors"):
        cads = [cad_t] + [swap(cad_t, "star", bit) for bit in range(1, m)]

    far = n // 2
    pieces = [star_t] + [None] * (n - 1)
    with jax.named_scope("gather_star_factors"):
        beside = swap(star_t, "star", 1)
        for s in range(1, far):
            pieces[s] = shift(pieces[s - 1])
            if s == 1:
                beside = shift(beside)
                pieces[s], beside = hold(pieces[s], light), hold(beside, light)
            elif s < far - 1:
                beside = shift(beside)
                pieces[s] = hold(pieces[s], *cads[1:])
            else:
                beside = shift(beside, 1)
            pieces[n - s] = swap(beside, "star", 1) if s < far - 1 else beside
        far_a, far_b = shift(pieces[far - 1][:, :half]), shift(pieces[far - 1][:, half:])

    slots = [k for k in range(n) if k not in (far, far + 1)]
    rest = early(light, [pieces[k] for k in slots], cads, star_slot, cad_slot, slots)
    late, lead = [far, far + 1], [far, far - 1, far - 2]
    got_a = cells(rest, quality, [far_a, pieces[far + 1]], cads, [], scale, star_slot, cad_slot, late, lead, 0, 2)
    got_b = cells(rest, quality, [far_b, pieces[far + 1]], cads, got_a[2:], scale, star_slot, cad_slot, late, lead, 1, 2)
    loss = got_b[2]
    pieces[far] = far_a
    slots = [k for k in range(n) if k not in lead]
    second, third = swap(got_b[4], "star", 1), swap(got_b[5], "star", 1)
    loss = hold(loss, second)
    got = sums(got_a[:2] + got_b[:2], loss, quality, pieces, [far_b], cads, scale, cad_scale, star_slot, cad_slot, slots)
    terms = dict(zip(lead + slots, got_b[3:] + got[:-2], strict=True))
    keep, send = got[-2:]

    with jax.named_scope("scatter_star_gradient"):
        up, beside = shift(terms[far]), shift(second)
        up = shift(terms[far + 1] + up)
        message = third + beside
        keep, send = halve(keep, swap(hold(send, message), "star", 2))
        beside = shift(message)
        up = shift(hold(terms[far + 2] + up, message))
        message = hold(swap(terms[1], "star", 1) + beside, keep)
        beside = shift(message, 1)
        message, near = add_part(terms[far + 3], hold(up, message))
        near = shift(near)
        up = shift(message)
        part = loss_part(loss, near, beside)
        part = add_losses([part, swap(part, "star", 1)])
        losses = [part, swap(part, "star", 2)]
        kept = [keep, swap(hold(send, beside), "star", 1)]
        star_gradient, cad_gradient, total = last_sums(terms[0], up, beside, kept, losses, factor)
    return (star_gradient.T, cad_gradient.T, total[0, 0])


def whole_program(light, quality, star_t, cad_t):
    n, m = lax.axis_size("cad"), lax.axis_size("star")
    count, nc = light.shape
    scale = -1.0 / float(nc * n) ** 0.5
    cad_scale = -1.0 / float(count * m) ** 0.5
    stars = [lax.all_gather(star_t, "cad", axis=0, tiled=True)]
    cads = [lax.all_gather(cad_t, "star", axis=0, tiled=True)]
    first = lambda k: 0
    light = early(light, stars, cads, first, first, [0])
    whi, wlo, loss = cells(light, quality.reshape(1, -1), [], cads, [], scale, first, first, [], [], 0, 1)
    parts = [whi, wlo]
    star, cad, _ = sums(parts, loss, quality.reshape(1, -1), stars, [], cads, scale, cad_scale, first, first, [0])
    star_gradient = lax.psum_scatter(star, "cad", scatter_dimension=0, tiled=True)
    cadence_gradient = lax.psum_scatter(cad, "star", scatter_dimension=0, tiled=True)
    loss = lax.psum(jnp.sum(loss), ("star", "cad")) * (2.0 / (float(count * m) * float(nc * n)))
    return (star_gradient.T, cadence_gradient.T, loss)


def on_device(light, quality, star_factors, cadence_factors):
    ring = lax.axis_size("cad") == 8 and lax.axis_size("star") == 4
    program = ring_program if ring else whole_program
    return program(light, quality, star_factors.T, cadence_factors.T)


def solution(mesh):
    in_specs = (P("star", "cad"), P("cad"), P("star", "cad"), P("cad", "star"))
    out_specs = (P("star", "cad"), P("cad", "star"), P())
    return jax.shard_map(
        on_device, mesh=mesh, in_specs=in_specs, out_specs=out_specs, check_vma=False
    )
```

```python
import functools

import jax
import jax.numpy as jnp
from jax import lax
from jax.experimental import pallas as pl
from jax.experimental.pallas import tpu as pltpu
from jax.sharding import PartitionSpec as P

F32 = jnp.float32
BF16 = jnp.bfloat16
SUB = 1024


def two(x):
    hi = x.astype(BF16)
    return hi, (x - hi.astype(F32)).astype(BF16)


def three(x):
    hi = x.astype(BF16)
    rest = x - hi.astype(F32)
    mid = rest.astype(BF16)
    return hi, mid, (rest - mid.astype(F32)).astype(BF16)


def mm(a, b, ca, cb):
    return lax.dot_general(a, b, (((ca,), (cb,)), ((), ())), preferred_element_type=F32)


def rank_rows(k, rows):
    return pl.ds(pl.multiple_of(k * rows, rows), rows)


def stage_body(*refs):
    count = len(refs) // 2
    sem = refs[-1]
    copies = [pltpu.make_async_copy(refs[i], refs[count + i], sem.at[i]) for i in range(count)]
    for copy in copies:
        copy.start()
    for copy in copies:
        copy.wait()


def stage(*given):
    return pl.pallas_call(
        stage_body,
        in_specs=[pl.BlockSpec(memory_space=pl.ANY)] * len(given),
        out_specs=[pl.BlockSpec(memory_space=pltpu.VMEM)] * len(given),
        out_shape=[jax.ShapeDtypeStruct(x.shape, x.dtype) for x in given],
        scratch_shapes=[pltpu.SemaphoreType.DMA((len(given),))],
        cost_estimate=pl.CostEstimate(flops=0, bytes_accessed=1 << 10, transcendentals=0),
        compiler_params=pltpu.CompilerParams(vmem_limit_bytes=16 << 20),
    )(*given)


def place_cads(whole, cads, cad_slot):
    rows = cads[0].shape[0]
    for k, ref in enumerate(cads):
        whole[rank_rows(cad_slot(k), rows), :] = ref[...]


def of_slots(whole, star_slot, slots, rows):
    return jnp.concatenate([whole[rank_rows(star_slot(k), rows), :] for k in slots], 0)


def columns(refs, start, size):
    return jnp.concatenate([ref[:, pl.ds(start, size)] for ref in refs], 0)


def product_left(s):
    hi, mid, lo = three(s)
    return jnp.concatenate([hi, lo, mid, mid, hi, hi], 0)


def product_right(c):
    hi, mid, lo = three(c)
    return jnp.concatenate([lo, hi, hi, mid, hi, mid], 0)


def early_body(plan, *refs):
    star_slot, cad_slot, slots, n_cad = plan
    light, refs = refs[0], refs[1:]
    stars, cads = refs[: len(slots)], refs[len(slots) : len(slots) + n_cad]
    out, whole = refs[-2:]
    rows = stars[0].shape[0]
    place_cads(whole, cads, cad_slot)
    pad = -rows * len(slots) % 128
    block = of_slots(whole, star_slot, slots, rows)
    if pad:
        block = jnp.concatenate([block, jnp.zeros((pad, block.shape[1]), F32)], 0)
    right = product_right(block)
    for start in range(0, light.shape[0], SUB):
        s = columns(stars, start, SUB)
        if pad:
            s = jnp.concatenate([s, jnp.zeros((pad, SUB), F32)], 0)
        hi, mid, lo = three(s.T)
        left = jnp.concatenate([hi, lo, mid, mid, hi, hi], 1)
        at = pl.ds(start, SUB)
        out[at, :] = light[at, :] - mm(left, right, 1, 0)


def cells_body(plan, *refs):
    scale, star_slot, cad_slot, late, lead, n_cad, offset, first, last = plan
    refs = list(refs)
    take = lambda count: [refs.pop(0) for _ in range(count)]
    rest, quality = take(2)
    stars, cads = take(len(late)), take(n_cad)
    before = [] if first else take(1 + len(lead))
    whi_out, wlo_out, loss_out = take(3)
    terms = take(len(lead))
    whole, lacc = refs
    width = whi_out.shape[0]
    good = quality[...].astype(F32)
    place_cads(whole, cads, cad_slot)
    rows = stars[0].shape[0] if late else 0
    right = product_right(of_slots(whole, star_slot, late, rows)) if late else None
    ghi, glo = two(of_slots(whole, star_slot, lead, rows) * (good * scale)) if lead else (None, None)
    gt = jnp.concatenate([glo.T, ghi.T, ghi.T], 0) if lead else None
    lacc[...] = jnp.zeros_like(lacc) if first else before[0][...]
    for start in range(0, width, SUB):
        at = pl.ds(start, SUB)
        residual = rest[pl.ds(offset + start, SUB), :]
        if late:
            s = jnp.concatenate([r[:, pl.ds((offset if r.shape[1] > width else 0) + start, SUB)] for r in stars], 0)
            residual = residual - mm(product_left(s), right, 0, 0)
        ratio = 1.0 + (residual * 0.5) ** 2
        whi, wlo = two(residual / ratio)
        whi_out[at, :], wlo_out[at, :] = whi, wlo
        if lead:
            term = mm(jnp.concatenate([whi, wlo, whi], 1), gt, 1, 0).T
            for k, ref in enumerate(terms):
                to = pl.ds(start if first else width + start, SUB)
                ref[:, to] = term[k * rows : (k + 1) * rows]
        q = SUB // 4
        prod = (ratio[:q] * ratio[q : 2 * q]) * (ratio[2 * q : 3 * q] * ratio[3 * q :])
        lacc[...] += jnp.sum(jnp.log(prod).reshape(q // 8, 8, -1), 0)
    if not last:
        loss_out[...] = lacc[...]
        return
    sums = lacc[...] * good
    lanes = sum(sums[:, c : c + 128] for c in range(0, sums.shape[1], 128))
    loss_out[...] = lanes
    for ref, half in zip(terms, before[1:], strict=True):
        ref[:, :width] = half[...]
        put_lanes(ref, lanes)


def put_lanes(ref, lanes):
    ref[:8, ref.shape[1] - 128 :] = lanes
    ref[8:, ref.shape[1] - 128 :] = jnp.zeros((ref.shape[0] - 8, 128), F32)


def sums_body(plan, *refs):
    scale, cad_scale, star_slot, cad_slot, slots, n_star, n_cad, chunks = plan
    refs = list(refs)
    take = lambda count: [refs.pop(0) for _ in range(count)]
    parts, loss, quality = take(2 * chunks), take(1)[0], take(1)[0]
    stars, halves, cads = take(n_star), take(chunks - 1), take(n_cad)
    outs = take(len(slots))
    keep, send, whole, acc = refs
    rows, crows = stars[0].shape[0], cads[0].shape[0]
    width = parts[0].shape[0]
    good = quality[...].astype(F32)
    place_cads(whole, cads, cad_slot)
    ghi, glo = two(of_slots(whole, star_slot, slots, rows) * (good * scale))
    gt = jnp.concatenate([glo.T, ghi.T, ghi.T], 0)
    acc[...] = jnp.zeros_like(acc)
    for c in range(chunks):
        pieces = list(stars)
        if c:
            pieces[n_star // 2] = halves[c - 1]
        for start in range(0, width, SUB):
            at = pl.ds(start, SUB)
            whi, wlo = parts[2 * c][at, :], parts[2 * c + 1][at, :]
            term = mm(jnp.concatenate([whi, wlo, whi], 1), gt, 1, 0).T
            for k, ref in enumerate(outs):
                ref[:, pl.ds(c * width + start, SUB)] = term[k * rows : (k + 1) * rows]
            s = jnp.concatenate([r[:, pl.ds((c * width if r.shape[1] > width else 0) + start, SUB)] for r in pieces], 0)
            shi, slo = two(s)
            acc[...] += mm(jnp.concatenate([slo, shi, shi], 1), jnp.concatenate([whi, wlo, whi], 0), 1, 0)
    if chunks > 1:
        for ref in outs:
            put_lanes(ref, loss[...])
    for k in range(n_star):
        whole[rank_rows(star_slot(k), rows), :] = acc[k * rows : (k + 1) * rows]
    mine = max(n_cad // 2, 1)
    for k in range(n_cad):
        ref, place = (keep, k) if k < mine else (send, k - mine)
        ref[pl.ds(place * crows, crows), :] = whole[rank_rows(cad_slot(k), crows), :] * (good * cad_scale)


def big_call(body_of, given, out_shape, scratch, macs):
    vmem = pl.BlockSpec(memory_space=pltpu.VMEM)
    return pl.pallas_call(
        body_of,
        in_specs=[vmem] * len(given),
        out_specs=[vmem] * len(out_shape),
        out_shape=out_shape,
        scratch_shapes=scratch,
        compiler_params=pltpu.CompilerParams(vmem_limit_bytes=24 << 20),
        cost_estimate=pl.CostEstimate(flops=2 * macs, bytes_accessed=1 << 20, transcendentals=0),
    )(*given)


def sds(*shape, kind=F32):
    return jax.ShapeDtypeStruct(shape, kind)


def early(light, stars, cads, star_slot, cad_slot, slots):
    count, nc = light.shape
    rank = cads[0].shape[0] * len(cads)
    plan = (star_slot, cad_slot, slots, len(cads))
    scratch = [pltpu.VMEM((rank, nc), F32)]
    return big_call(functools.partial(early_body, plan), [light] + stars + cads, [sds(count, nc)], scratch, 6 * count * nc * rank)[0]


def cells(rest, quality, stars, cads, before, scale, star_slot, cad_slot, late, lead, chunk, chunks):
    count, nc = rest.shape
    width = count // chunks
    rank = cads[0].shape[0] * len(cads)
    rows = stars[0].shape[0] if stars else 0
    first, last = chunk == 0, chunk == chunks - 1
    plan = (scale, star_slot, cad_slot, late, lead, len(cads), chunk * width, first, last)
    out = [sds(width, nc, kind=BF16)] * 2 + [sds(8, 128) if last else sds(8, nc)]
    out += [sds(rows, width if first else count + 128)] * len(lead)
    scratch = [pltpu.VMEM((rank, nc), F32), pltpu.VMEM((8, nc), F32)]
    return list(big_call(functools.partial(cells_body, plan), [rest, quality] + stars + cads + before, out, scratch, 4 * width * nc * rank))


def sums(parts, loss, quality, stars, halves, cads, scale, cad_scale, star_slot, cad_slot, slots):
    chunks, nc = len(parts) // 2, parts[0].shape[1]
    count = parts[0].shape[0] * chunks
    n_star, n_cad = len(stars), len(cads)
    rows, crows = stars[0].shape[0], cads[0].shape[0]
    rank = rows * n_star
    mine = max(n_cad // 2, 1)
    plan = (scale, cad_scale, star_slot, cad_slot, slots, n_star, n_cad, chunks)
    out = [sds(rows, count + (128 if chunks > 1 else 0))] * len(slots)
    out += [sds(crows * mine, nc), sds(crows * max(n_cad - mine, 1), nc)]
    scratch = [pltpu.VMEM((rank, nc), F32), pltpu.VMEM((rank, nc), F32)]
    given = parts + [loss, quality] + stars + halves + cads
    return list(big_call(functools.partial(sums_body, plan), given, out, scratch, 6 * count * nc * rank))


def small_call(body_of, given, shapes, weight=0):
    vmem = pl.BlockSpec(memory_space=pltpu.VMEM)
    return pl.pallas_call(
        body_of,
        in_specs=[vmem] * len(given),
        out_specs=[vmem] * len(shapes),
        out_shape=[jax.ShapeDtypeStruct(shape, F32) for shape in shapes],
        cost_estimate=pl.CostEstimate(flops=weight, bytes_accessed=1 << 10, transcendentals=0),
        compiler_params=pltpu.CompilerParams(vmem_limit_bytes=4 << 20),
    )(*given)


def empty_body(*refs):
    pass


def hold(x, *after):
    anywhere = pl.BlockSpec(memory_space=pl.ANY)
    return pl.pallas_call(
        empty_body,
        in_specs=[anywhere] * (1 + len(after)),
        out_specs=anywhere,
        out_shape=jax.ShapeDtypeStruct(x.shape, x.dtype),
        input_output_aliases={0: 0},
        cost_estimate=pl.CostEstimate(flops=0, bytes_accessed=1 << 10, transcendentals=0),
        compiler_params=pltpu.CompilerParams(vmem_limit_bytes=1 << 20),
    )(x, *after)


def halve_body(keep, got, keep_out, send_out):
    rows = keep_out.shape[0]
    keep_out[...] = keep[:rows] + got[:rows]
    send_out[...] = keep[rows:] + got[rows:]


def halve(keep, got):
    shape = (keep.shape[0] // 2, keep.shape[1])
    return small_call(halve_body, [keep, got], [shape, shape])


def add_part_body(mine, got, out, part):
    width = out.shape[1]
    out[...] = mine[:, :width] + got[:, :width]
    part[...] = mine[:8, width:] + got[:8, width:]


def add_part(mine, got):
    return small_call(add_part_body, [mine, got], [(mine.shape[0], mine.shape[1] - 128), (8, 128)])


def loss_part_body(loss, near, beside, out):
    out[...] = loss[...] + near[...] + beside[:8, beside.shape[1] - 128 :]


def loss_part(loss, near, beside):
    return small_call(loss_part_body, [loss, near, beside], [(8, 128)], weight=3 * 10**9)[0]


def add_losses_body(*refs):
    refs[-1][...] = sum(ref[...] for ref in refs[:-1])


def add_losses(losses):
    return small_call(add_losses_body, losses, [(8, 128)])[0]


def last_sums_body(factor, mine, up, back, keep, got, *refs):
    *losses, out, cad_out, total = refs
    width = out.shape[1]
    out[...] = mine[:, :width] + up[:, :width] + back[:, :width]
    cad_out[...] = keep[...] + got[...]
    total[...] = jnp.sum(sum(ref[...] for ref in losses), keepdims=True) * factor


def last_sums(mine, up, back, kept, losses, factor):
    rows, width = mine.shape
    shapes = [(rows, width - 128), kept[0].shape, (1, 1)]
    return small_call(functools.partial(last_sums_body, factor), [mine, up, back] + kept + losses, shapes)


def ring_order(n):
    return list(range(0, n, 2)) + list(range(1, n, 2))[::-1]


def shift(x, core=0, places=1):
    m, n = lax.axis_size("star"), lax.axis_size("cad")
    order = ring_order(n)
    pairs = []
    for i in range(m):
        way = places if i % 2 == 0 else -places
        source, target = i ^ int(core < 0), i ^ int(core > 0)
        pairs += [(source * n + order[p], target * n + order[(p + way) % n]) for p in range(n)]
    return lax.ppermute(x, ("star", "cad"), pairs)


def swap(x, axis, bit):
    return lax.ppermute(x, axis, [(i, i ^ bit) for i in range(lax.axis_size(axis))])


def ring_program(light, quality, star_t, cad_t):
    n, m = lax.axis_size("cad"), lax.axis_size("star")
    count, nc = light.shape
    half = count // 2
    scale = -1.0 / float(nc * n) ** 0.5
    cad_scale = -1.0 / float(count * m) ** 0.5
    factor = 2.0 / (float(count * m) * float(nc * n))

    def star_slot(k):
        me = lax.axis_index("cad")
        place = jnp.where(me % 2 == 0, me // 2, n - 1 - me // 2)
        back = jnp.where(lax.axis_index("star") % 2 == 0, n - k, k)
        source = lax.rem(place + back, n)
        return jnp.where(source < n // 2, 2 * source, 2 * (n - 1 - source) + 1)

    def cad_slot(k):
        return jnp.bitwise_xor(lax.axis_index("star"), k)

    light = stage(light)[0]
    quality = quality.reshape(1, -1)

    with jax.named_scope("gather_cadence_factors"):
        cads = [cad_t] + [swap(cad_t, "star", bit) for bit in range(1, m)]

    far = n // 2
    pieces = [star_t] + [None] * (n - 1)
    with jax.named_scope("gather_star_factors"):
        beside = swap(star_t, "star", 1)
        for s in range(1, far):
            pieces[s] = shift(pieces[s - 1])
            if s == 1:
                beside = shift(beside)
                pieces[s], beside = hold(pieces[s], light, cads[1]), hold(beside, light)
            elif s < far - 1:
                beside = shift(beside)
                pieces[s] = hold(pieces[s], *cads[1:])
            else:
                beside = shift(beside, 1)
            pieces[n - s] = swap(beside, "star", 1) if s < far - 1 else beside
        far_a, far_b = shift(pieces[far - 1][:, :half]), shift(pieces[far - 1][:, half:])

    slots = [k for k in range(n) if k not in (far, far + 1)]
    rest = early(light, [pieces[k] for k in slots], cads, star_slot, cad_slot, slots)
    late, lead = [far, far + 1], [far, far - 1, far - 2]
    got_a = cells(rest, quality, [far_a, pieces[far + 1]], cads, [], scale, star_slot, cad_slot, late, lead, 0, 2)
    got_b = cells(rest, quality, [far_b, pieces[far + 1]], cads, got_a[2:], scale, star_slot, cad_slot, late, lead, 1, 2)
    loss = got_b[2]
    pieces[far] = far_a
    slots = [k for k in range(n) if k not in lead]
    second, third = swap(got_b[4], "star", 1), swap(got_b[5], "star", 1)
    loss = hold(loss, second)
    got = sums(got_a[:2] + got_b[:2], loss, quality, pieces, [far_b], cads, scale, cad_scale, star_slot, cad_slot, slots)
    terms = dict(zip(lead + slots, got_b[3:] + got[:-2], strict=True))
    keep, send = got[-2:]

    with jax.named_scope("scatter_star_gradient"):
        up, beside = shift(terms[far]), shift(second)
        up = shift(terms[far + 1] + up)
        message = third + beside
        keep, send = halve(keep, swap(hold(send, message), "star", 2))
        beside = shift(message)
        up = shift(hold(terms[far + 2] + up, message))
        message = hold(swap(terms[1], "star", 1) + beside, keep)
        beside = shift(message, 1)
        message, near = add_part(terms[far + 3], hold(up, message))
        near = shift(near)
        up = shift(message)
        part = loss_part(loss, near, beside)
        part = add_losses([part, swap(part, "star", 1)])
        losses = [part, swap(part, "star", 2)]
        kept = [keep, swap(hold(send, beside), "star", 1)]
        star_gradient, cad_gradient, total = last_sums(terms[0], up, beside, kept, losses, factor)
    return (star_gradient.T, cad_gradient.T, total[0, 0])


def whole_program(light, quality, star_t, cad_t):
    n, m = lax.axis_size("cad"), lax.axis_size("star")
    count, nc = light.shape
    scale = -1.0 / float(nc * n) ** 0.5
    cad_scale = -1.0 / float(count * m) ** 0.5
    stars = [lax.all_gather(star_t, "cad", axis=0, tiled=True)]
    cads = [lax.all_gather(cad_t, "star", axis=0, tiled=True)]
    first = lambda k: 0
    light = early(light, stars, cads, first, first, [0])
    whi, wlo, loss = cells(light, quality.reshape(1, -1), [], cads, [], scale, first, first, [], [], 0, 1)
    parts = [whi, wlo]
    star, cad, _ = sums(parts, loss, quality.reshape(1, -1), stars, [], cads, scale, cad_scale, first, first, [0])
    star_gradient = lax.psum_scatter(star, "cad", scatter_dimension=0, tiled=True)
    cadence_gradient = lax.psum_scatter(cad, "star", scatter_dimension=0, tiled=True)
    loss = lax.psum(jnp.sum(loss), ("star", "cad")) * (2.0 / (float(count * m) * float(nc * n)))
    return (star_gradient.T, cadence_gradient.T, loss)


def on_device(light, quality, star_factors, cadence_factors):
    ring = lax.axis_size("cad") == 8 and lax.axis_size("star") == 4
    program = ring_program if ring else whole_program
    return program(light, quality, star_factors.T, cadence_factors.T)


def solution(mesh):
    in_specs = (P("star", "cad"), P("cad"), P("star", "cad"), P("cad", "star"))
    out_specs = (P("star", "cad"), P("cad", "star"), P())
    return jax.shard_map(
        on_device, mesh=mesh, in_specs=in_specs, out_specs=out_specs, check_vma=False
    )
```
